32 devices in a mesh: section: 4 (over y, core), ctx: 8 (over z, x).
Axes of the slice: x: 2, y: 2, z: 4, core: 2. Of those that a mesh axis runs over, the one named last changes fastest.
Arguments:
- query_rows: bfloat16 [4096, 4096], P(('section', 'ctx')), may hold values from -6 to 6
- key_rows: bfloat16 [4096, 4096], P(('section', 'ctx')), may hold values from -6 to 6
- value_rows: bfloat16 [4096, 4096], P(('section', 'ctx')), may hold values from -6 to 6
- short_taps: bfloat16 [4, 3, 3, 4096], P('section', None, None, 'ctx'), may hold values from -3 to 3
- long_taps: bfloat16 [4, 4096, 128], P('section', 'ctx'), may hold values from -0.5 to 0.5
- skip_gain: bfloat16 [4, 4096], P('section', 'ctx'), may hold values from 0.5 to 1.5
- prior_qkv: bfloat16 [4, 3, 2, 4096], P('section', None, None, 'ctx'), may hold values from -6 to 6
- prior_product: bfloat16 [4, 127, 4096], P('section', None, 'ctx'), may hold values from -6 to 6
Outputs:
- handed: bfloat16 [4096, 4096], P(('section', 'ctx'))
The draws below stay inside these ranges and needn't reach their ends.
All inputs are finite; a program needn't handle non-finite values.
Results may differ from the reference program's by a relative error of at most 0.005.
Values may be sent and summed in bfloat16 or wider, within the bound.
A program may use at most 128 MiB of HBM per device.

```python
import jax
import jax.numpy as jnp
from jax import lax

C = 4096
TAPS = 128
SHORT = 3
LENGTH = 1024
ROWS = 4096
N_SECTION = 4


def block_levels(rng, dims, cuts, low, top_value):
    def one(dim, shards_of):
        draws = jax.random.uniform(jax.random.fold_in(jax.random.fold_in(rng, 6), dim), (shards_of,), jnp.float32, low / len(cuts), top_value / len(cuts))
        return jnp.repeat(jnp.exp(draws), dims[dim] // shards_of).reshape((-1,) + (1,) * (len(dims) - dim - 1))

    factor_of = one(*cuts[0])
    for cut in cuts[1:]:
        factor_of = factor_of * one(*cut)
    return factor_of


def scatter_about(rng, dims, scale, reach, shards=(), kind=jnp.bfloat16):
    result = jax.random.normal(rng, dims, jnp.float32) * scale
    if len(shards) > 0:
        result = block_levels(rng, dims, shards, -0.22, 0.18) * result
    return jnp.clip(result, min=-reach, max=reach).astype(kind)


def setup_inputs(seed: int = 0) -> dict:
    arg_keys = jax.random.split(jax.random.key(seed), 9)
    query_rows = scatter_about(arg_keys[0], (ROWS, C), 1.0, 6.0, ((0, 32),))
    key_rows = scatter_about(arg_keys[1], (ROWS, C), 1.0, 6.0, ((0, 32),))
    value_rows = scatter_about(arg_keys[2], (ROWS, C), 1.0, 6.0, ((0, 32),))
    short_taps = scatter_about(arg_keys[3], (N_SECTION, 3, SHORT, C), 0.6, 3.0, ((0, 4), (3, 8)))
    long_taps = scatter_about(arg_keys[4], (N_SECTION, C, TAPS), 0.088, 0.5, ((0, 4), (1, 8)))
    skip_gain = jnp.clip(1.0 + 0.1 * jax.random.normal(arg_keys[5], (N_SECTION, C), jnp.float32), 0.5, 1.5).astype(jnp.bfloat16)
    prior_qkv = scatter_about(arg_keys[6], (N_SECTION, 3, 2, C), 1.0, 6.0, ((0, 4), (3, 8)))
    prior_product = scatter_about(arg_keys[7], (N_SECTION, 127, C), 1.0, 6.0, ((0, 4), (2, 8)))
    return dict(query_rows=query_rows, key_rows=key_rows, value_rows=value_rows, short_taps=short_taps, long_taps=long_taps, skip_gain=skip_gain, prior_qkv=prior_qkv, prior_product=prior_product)


def featurize(rows, history, taps):
    padded = jnp.concatenate([history, rows], axis=0).astype(jnp.float32)
    weights = taps.astype(jnp.float32)
    return weights[0] * padded[2:] + weights[1] * padded[1:-1] + weights[2] * padded[:-2]


def one_section(pieces):
    query_rows, key_rows, value_rows, short_taps, long_taps, skip_gain, prior_qkv, prior_product = pieces
    query_feat = featurize(query_rows, prior_qkv[0], short_taps[0])
    key_feat = featurize(key_rows, prior_qkv[1], short_taps[1])
    value_feat = featurize(value_rows, prior_qkv[2], short_taps[2])
    product = (key_feat * value_feat).astype(jnp.bfloat16)
    product_f = product.astype(jnp.float32)
    extended = jnp.concatenate([prior_product.astype(jnp.float32), product_f], axis=0)
    spectrum = jnp.fft.rfft(extended, n=2 * LENGTH, axis=0) * jnp.fft.rfft(long_taps.astype(jnp.float32).T, n=2 * LENGTH, axis=0)
    filtered = jnp.fft.irfft(spectrum, n=2 * LENGTH, axis=0)[127:127 + LENGTH].astype(jnp.float32)
    mixed = query_feat * (filtered + skip_gain.astype(jnp.float32) * product_f)
    return mixed.astype(jnp.bfloat16)


def reference(query_rows, key_rows, value_rows, short_taps, long_taps, skip_gain, prior_qkv, prior_product):
    shape = (N_SECTION, LENGTH, C)
    mixed = lax.map(one_section, (query_rows.reshape(shape), key_rows.reshape(shape), value_rows.reshape(shape), short_taps, long_taps, skip_gain, prior_qkv, prior_product))
    handed = jnp.concatenate([mixed[-1:], mixed[:-1]], axis=0)
    return handed.reshape(N_SECTION * LENGTH, C)
```

```python
import functools

import jax
import jax.numpy as jnp
import numpy as np
from jax import lax
from jax.experimental import pallas as pl
from jax.experimental.pallas import tpu as pltpu
from jax.sharding import PartitionSpec as P

MESH = pl.DeviceIdType.MESH
F32 = jnp.float32
BF16 = jnp.bfloat16


def transforms(block):
    size = 2 * block
    freq = (2 * np.arange(block)[:, None] + 1).astype(np.int64)
    turn = np.pi * ((freq * np.arange(size)[None, :]) % (2 * size)) / size
    forward = np.concatenate([np.cos(turn), -np.sin(turn)], axis=0)
    inverse = (forward * (2.0 / size)).T[block:]

    def two_terms(matrix):
        high = matrix.astype(jnp.bfloat16)
        low = (matrix - high.astype(np.float64)).astype(jnp.bfloat16)
        return np.stack([high, low])

    return two_terms(forward), two_terms(inverse)


def dot(a, b):
    return jnp.dot(a, b, preferred_element_type=F32)


def kernel(
    n_section, n_ctx,
    q_hbm, k_hbm, v_hbm, short_ref, taps_ref, gain_ref, prior_ref, tail_ref, fwd_ref, inv_ref,
    out_ref,
    q_ref, k_ref, v_ref, own_msg, msgs, taps_all, own_tail, edge_out, edge_in, edges,
    p_out, p_own, p_in, hist, prev, f_out, f_in, mixed,
    load_sem, msg_send, msg_recv, taps_send, taps_recv, tail_send, hist_send, hist_recv,
    edge_send, edge_recv, p_send, p_recv, f_send, f_recv, out_send, out_recv,
):
    section = lax.axis_index("section")
    me = lax.axis_index("ctx")
    rows_of = n_ctx // 2
    z, x = me // 2, me % 2
    partner = me + 1 - 2 * x
    after = lax.rem(section + 1, n_section)
    before = lax.rem(section + n_section - 1, n_section)
    block, channels = q_ref.shape
    width = channels // n_ctx
    half = channels // 2

    loads = [
        pltpu.make_async_copy(src, dst, load_sem.at[i])
        for i, (src, dst) in enumerate(((q_hbm, q_ref), (k_hbm, k_ref), (v_hbm, v_ref)))
    ]
    for load in loads:
        load.start()

    barrier = pltpu.get_barrier_semaphore()
    for step in range(1, n_ctx):
        pl.semaphore_signal(
            barrier, inc=1, device_id={"ctx": lax.rem(me + step, n_ctx)}, device_id_type=MESH
        )
    for other in (after, before):
        pl.semaphore_signal(barrier, inc=1, device_id={"section": other}, device_id_type=MESH)

    pieces = [short_ref[0, m].astype(F32) for m in range(3)]
    pieces += [prior_ref[0, m].astype(F32) for m in range(3)]
    pieces.append(gain_ref[...].astype(F32))
    own_msg[...] = jnp.concatenate(pieces, axis=0).astype(BF16)
    msgs[me] = own_msg[...]
    own_tail[...] = jnp.concatenate(
        [jnp.zeros((1, width), F32), tail_ref[0].astype(F32)], axis=0
    ).astype(BF16)
    taps_all[z] = taps_ref[0]

    @pl.when(z == 0)
    def _():
        hist[0] = own_tail[...]

    for load in loads:
        load.wait()
    last = [ref[block - 16:, :].astype(F32)[14:] for ref in (q_ref, k_ref, v_ref)]
    edge_out[...] = jnp.concatenate(
        [piece[:, :half] for piece in last]
        + [piece[:, half:] for piece in last]
        + [jnp.zeros((4, half), F32)],
        axis=0,
    ).astype(BF16)

    pl.semaphore_wait(barrier, n_ctx + 1)

    def remote(src, dst, send, recv, **where):
        return pltpu.make_async_remote_copy(
            src_ref=src, dst_ref=dst, send_sem=send, recv_sem=recv,
            device_id=where, device_id_type=MESH,
        )

    def edge_copy():
        return remote(edge_out, edge_in, edge_send, edge_recv, ctx=lax.rem(me + 1, n_ctx))

    def msg_copy(step, slot):
        return remote(
            own_msg, msgs.at[slot], msg_send.at[step], msg_recv.at[step],
            ctx=lax.rem(me + step, n_ctx),
        )

    def taps_copy(step, slot):
        return remote(
            taps_ref.at[0], taps_all.at[slot], taps_send.at[step], taps_recv.at[step],
            ctx=lax.rem(z + step, rows_of) * 2 + x,
        )

    def tail_copy():
        return remote(own_tail, hist.at[z], tail_send, hist_recv.at[z], ctx=x)

    def hist_copy(src, i):
        return remote(
            src.at[i], hist.at[i], hist_send.at[i], hist_recv.at[i],
            ctx=lax.rem(me + 2, n_ctx),
        )

    def p_copy(i):
        return remote(p_out.at[i], p_in.at[i], p_send.at[i], p_recv.at[i], ctx=partner)

    def f_copy(i):
        return remote(f_out.at[i], f_in.at[i], f_send.at[i], f_recv.at[i], ctx=partner)

    def columns(c):
        return pl.ds(pl.multiple_of(c * width, 128), width)

    def out_copy(c):
        return remote(
            mixed.at[:, columns(c)], out_ref.at[:, columns(c)], out_send.at[c], out_recv.at[c],
            section=after,
        )

    @pl.when(me < n_ctx - 1)
    def _():
        edge_copy().start()

    for step in range(1, n_ctx):
        msg_copy(step, me).start()
    for step in range(1, rows_of):
        taps_copy(step, z).start()

    @pl.when(z > 0)
    def _():
        tail_copy().start()

    for step in range(1, n_ctx):
        msg_copy(step, lax.rem(me - step + n_ctx, n_ctx)).wait_recv()

    @pl.when(me > 0)
    def _():
        edge_copy().wait_recv()
        got = edge_in[...].astype(F32)
        edges[0:6, :half] = got[0:6]
        edges[0:6, half:] = got[6:12]

    @pl.when(me == 0)
    def _():
        def place(c, carry):
            edges[0:6, columns(c)] = msgs[c].astype(F32)[9:15]
            return carry

        lax.fori_loop(0, n_ctx, place, 0)

    def feature(ref, c, lane, m, message):
        at = pl.ds(pl.multiple_of(c * width + lane, 128), 128)
        rows = ref[:, at].astype(F32)
        ends = edges[:, at]
        older, newer = ends[2 * m : 2 * m + 1], ends[2 * m + 1 : 2 * m + 2]
        place = lax.broadcasted_iota(jnp.int32, rows.shape, 0)
        one = jnp.where(place == 0, newer, pltpu.roll(rows, 1, 0))
        two = jnp.where(
            place == 0, older, jnp.where(place == 1, newer, pltpu.roll(rows, 2, 0))
        )
        weights = message[3 * m : 3 * m + 3, lane : lane + 128]
        return weights[0:1] * rows + weights[1:2] * one + weights[2:3] * two

    def product(c, dst, i):
        message = msgs[c].astype(F32)
        for lane in range(0, width, 128):
            key = feature(k_ref, c, lane, 1, message)
            value = feature(v_ref, c, lane, 2, message)
            dst[i, :, lane : lane + 128] = (key * value).astype(BF16)

    def partner_products(i, carry):
        product(2 * i + 1 - x, p_out, i)
        p_copy(i).start()
        return carry

    lax.fori_loop(0, rows_of, partner_products, 0)

    def own_products(i, carry):
        product(2 * i + x, p_own, i)

        @pl.when((x == 1) & (z < rows_of - 1))
        def _():
            hist_copy(p_own, i).start()

        return carry

    lax.fori_loop(0, rows_of, own_products, 0)

    def finish(c, filtered):
        message = msgs[c].astype(F32)
        for lane in range(0, width, 128):
            at = pl.ds(pl.multiple_of(c * width + lane, 128), 128)
            query = feature(q_ref, c, lane, 0, message)
            mixed[:, at] = (query * filtered[:, lane : lane + 128]).astype(BF16)
        out_copy(c).start()

    def from_partner(i):
        f_copy(i).wait_recv()
        finish(2 * i + 1 - x, f_in[i].astype(F32))

    def spectrum(window):
        return dot(fwd_ref[0], window) + dot(fwd_ref[1], window)

    def filtered_block(current, real, imag):
        window = spectrum(jnp.concatenate([prev[...], current], axis=0))
        one, two = window[:block], window[block:]
        result = jnp.concatenate([one * real - two * imag, one * imag + two * real], axis=0)
        high = result.astype(BF16)
        low = (result - high.astype(F32)).astype(BF16)
        return dot(inv_ref[0], high) + (dot(inv_ref[1], high) + dot(inv_ref[0], low))

    def wait_hist(i):
        @pl.when((z > 0) | (i > 0))
        def _():
            hist_copy(p_own, i).wait_recv()

    def main(i, carry):
        @pl.when(i != z)
        def _():
            step = lax.rem(z - i + rows_of, rows_of)
            taps_copy(step, i).wait_recv()

        taps = taps_all[i]
        over = (((1,), (1,)), ((), ()))
        response = lax.dot_general(
            fwd_ref[0, :, :block], taps, over, preferred_element_type=F32
        ) + lax.dot_general(fwd_ref[1, :, :block], taps, over, preferred_element_type=F32)
        gain = msgs[2 * i + x].astype(F32)[15:16]
        real, imag = response[:block] + gain, response[block:]

        p_copy(i).wait_recv()

        @pl.when((x == 0) & (z < rows_of - 1))
        def _():
            hist_copy(p_in, i).start()

        @pl.when(x == 0)
        def _():
            prev[...] = p_own[i]

        @pl.when(x == 1)
        def _():
            wait_hist(i)
            prev[...] = hist[i]

        f_out[i] = filtered_block(p_in[i], real, imag).astype(BF16)
        f_copy(i).start()

        @pl.when(x == 0)
        def _():
            wait_hist(i)
            prev[...] = hist[i]

        @pl.when(x == 1)
        def _():
            prev[...] = p_in[i]

        finish(2 * i + x, filtered_block(p_own[i], real, imag))

        @pl.when(i > 0)
        def _():
            from_partner(i - 1)

        return carry

    lax.fori_loop(0, rows_of, main, 0)
    from_partner(rows_of - 1)

    @pl.when(me < n_ctx - 1)
    def _():
        edge_copy().wait_send()

    for step in range(1, n_ctx):
        msg_copy(step, me).wait_send()
    for step in range(1, rows_of):
        taps_copy(step, z).wait_send()

    @pl.when(z > 0)
    def _():
        tail_copy().wait_send()

    def drain(i, carry):
        p_copy(i).wait_send()
        f_copy(i).wait_send()

        @pl.when(z < rows_of - 1)
        def _():
            hist_copy(p_own, i).wait_send()

        return carry

    lax.fori_loop(0, rows_of, drain, 0)

    def drain_out(c, carry):
        out_copy(c).wait()
        return carry

    lax.fori_loop(0, n_ctx, drain_out, 0)


def body(n_section, n_ctx, query, key, value, short_taps, long_taps, skip_gain, prior_qkv, prior_product):
    block, channels = query.shape
    width = channels // n_ctx
    rows_of = n_ctx // 2
    forward, inverse = transforms(block)
    hbm = pl.BlockSpec(memory_space=pl.ANY)
    vmem = pl.BlockSpec(memory_space=pltpu.VMEM)
    slots = (rows_of, block, width)
    sems = pltpu.SemaphoreType.DMA
    return pl.pallas_call(
        functools.partial(kernel, n_section, n_ctx),
        out_shape=jax.ShapeDtypeStruct(query.shape, BF16),
        in_specs=[hbm] * 3 + [vmem] * 7,
        out_specs=hbm,
        scratch_shapes=[
            pltpu.VMEM((block, channels), BF16),
            pltpu.VMEM((block, channels), BF16),
            pltpu.VMEM((block, channels), BF16),
            pltpu.VMEM((16, width), BF16),
            pltpu.VMEM((n_ctx, 16, width), BF16),
            pltpu.VMEM((rows_of, width, block), BF16),
            pltpu.VMEM((block, width), BF16),
            pltpu.VMEM((16, channels // 2), BF16),
            pltpu.VMEM((16, channels // 2), BF16),
            pltpu.VMEM((8, channels), F32),
            pltpu.VMEM(slots, BF16),
            pltpu.VMEM(slots, BF16),
            pltpu.VMEM(slots, BF16),
            pltpu.VMEM(slots, BF16),
            pltpu.VMEM((block, width), BF16),
            pltpu.VMEM(slots, BF16),
            pltpu.VMEM(slots, BF16),
            pltpu.VMEM((block, channels), BF16),
            sems((3,)),
            sems((n_ctx,)),
            sems((n_ctx,)),
            sems((rows_of,)),
            sems((rows_of,)),
            sems,
            sems((rows_of,)),
            sems((rows_of,)),
            sems,
            sems,
            sems((rows_of,)),
            sems((rows_of,)),
            sems((rows_of,)),
            sems((rows_of,)),
            sems((n_ctx,)),
            sems((n_ctx,)),
        ],
        compiler_params=pltpu.CompilerParams(
            collective_id=0, has_side_effects=True, vmem_limit_bytes=40 * 1024 * 1024
        ),
        cost_estimate=pl.CostEstimate(
            flops=2 * 2 * 256 * 256 * 4096, bytes_accessed=6 * 2**20, transcendentals=0
        ),
        name="paired_filter",
    )(
        query, key, value, short_taps, long_taps, skip_gain, prior_qkv, prior_product,
        jnp.asarray(forward), jnp.asarray(inverse),
    )


def solution(mesh):
    in_specs = (
        P(("section", "ctx"), None),
        P(("section", "ctx"), None),
        P(("section", "ctx"), None),
        P("section", None, None, "ctx"),
        P("section", "ctx", None),
        P("section", "ctx"),
        P("section", None, None, "ctx"),
        P("section", None, "ctx"),
    )
    out_specs = P(("section", "ctx"), None)
    run = functools.partial(body, mesh.shape["section"], mesh.shape["ctx"])
    return jax.shard_map(run, mesh=mesh, in_specs=in_specs, out_specs=out_specs, check_vma=False)
```

```python
import functools

import jax
import jax.numpy as jnp
import numpy as np
from jax import lax
from jax.experimental import pallas as pl
from jax.experimental.pallas import tpu as pltpu
from jax.sharding import PartitionSpec as P

MESH = pl.DeviceIdType.MESH
F32 = jnp.float32
BF16 = jnp.bfloat16
CHUNK = 512
VMEM_BYTES = 64 * 1024 * 1024


def transforms(block):
    size = 2 * block
    freq = (2 * np.arange(block)[:, None] + 1).astype(np.int64)
    turn = np.pi * ((freq * np.arange(size)[None, :]) % (2 * size)) / size
    forward = np.concatenate([np.cos(turn), -np.sin(turn)], axis=0)
    inverse = (forward * (2.0 / size)).T[block:]

    return forward.astype(np.float32), inverse.astype(np.float32)


def two_terms(matrix):
    high = matrix.astype(BF16)
    return high, (matrix - high.astype(F32)).astype(BF16)


def dot(a, b):
    return jnp.dot(a, b, preferred_element_type=F32)


def kernel(
    n_section, n_ctx,
    q_hbm, k_hbm, v_hbm, short_hbm, taps_hbm, gain_hbm, prior_hbm, tail_hbm, fwd_hbm, inv_hbm,
    out_ref,
    q_ref, k_ref, v_ref, short_ref, gain_ref, prior_ref, tail_ref, fwd_f32, inv_f32, fwd_ref, inv_ref, own_msg, msgs, taps_all, own_tail, edge_out, edge_in, edges,
    p_out, p_own, p_in, hist, prev, f_out, f_in, mixed,
    load_sem, msg_send, msg_recv, taps_send, taps_recv, tail_send, hist_send, hist_recv,
    edge_send, edge_recv, p_send, p_recv, f_send, f_recv, out_send, out_recv,
):
    section = lax.axis_index("section")
    me = lax.axis_index("ctx")
    rows_of = n_ctx // 2
    z, x = me // 2, me % 2
    partner = me + 1 - 2 * x
    after = lax.rem(section + 1, n_section)
    before = lax.rem(section + n_section - 1, n_section)
    block, channels = q_ref.shape
    width = channels // n_ctx
    half = channels // 2

    sub = p_out.shape[2]
    parts = width // sub

    loads = [
        pltpu.make_async_copy(src, dst, load_sem.at[i])
        for i, (src, dst) in enumerate(
            (
                (short_hbm, short_ref), (prior_hbm, prior_ref), (gain_hbm, gain_ref),
                (tail_hbm, tail_ref), (k_hbm, k_ref), (v_hbm, v_ref), (q_hbm, q_ref),
                (taps_hbm.at[0], taps_all.at[z]), (fwd_hbm, fwd_f32), (inv_hbm, inv_f32),
            )
        )
    ]
    for load in loads:
        load.start()

    barrier = pltpu.get_barrier_semaphore()
    for step in range(1, n_ctx):
        pl.semaphore_signal(
            barrier, inc=1, device_id={"ctx": lax.rem(me + step, n_ctx)}, device_id_type=MESH
        )
    for other in (after, before):
        pl.semaphore_signal(barrier, inc=1, device_id={"section": other}, device_id_type=MESH)

    for load in loads[:4]:
        load.wait()
    pieces = [short_ref[0, m].astype(F32) for m in range(3)]
    pieces += [prior_ref[0, m].astype(F32) for m in range(3)]
    pieces.append(gain_ref[...].astype(F32))
    own_msg[...] = jnp.concatenate(pieces, axis=0).astype(BF16)
    msgs[me] = own_msg[...]
    tail = jnp.concatenate(
        [jnp.zeros((1, width), F32), tail_ref[0].astype(F32)], axis=0
    ).astype(BF16)
    for part in range(parts):
        own_tail[part] = tail[:, part * sub : (part + 1) * sub]

    @pl.when(z == 0)
    def _():
        for part in range(parts):
            hist[part] = own_tail[part]

    for load in loads[4:7]:
        load.wait()
    last = [ref[block - 16:, :].astype(F32)[14:] for ref in (q_ref, k_ref, v_ref)]
    edge_out[...] = jnp.concatenate(
        [piece[:, :half] for piece in last]
        + [piece[:, half:] for piece in last]
        + [jnp.zeros((4, half), F32)],
        axis=0,
    ).astype(BF16)

    pl.semaphore_wait(barrier, n_ctx + 1)

    def remote(src, dst, send, recv, **where):
        return pltpu.make_async_remote_copy(
            src_ref=src, dst_ref=dst, send_sem=send, recv_sem=recv,
            device_id=where, device_id_type=MESH,
        )

    chunks = rows_of * parts
    partner_step = lax.rem(partner - me + n_ctx, n_ctx)

    def edge_copy():
        return remote(edge_out, edge_in, edge_send, edge_recv, ctx=lax.rem(me + 1, n_ctx))

    def msg_copy(step, slot):
        return remote(
            own_msg, msgs.at[slot], msg_send.at[step], msg_recv.at[step],
            ctx=lax.rem(me + step, n_ctx),
        )

    def taps_copy(step, slot):
        return remote(
            taps_hbm.at[0], taps_all.at[slot], taps_send.at[step], taps_recv.at[step],
            ctx=lax.rem(z + step, rows_of) * 2 + x,
        )

    def tail_copy(part):
        slot = z * parts + part
        return remote(
            own_tail.at[part], hist.at[slot], tail_send.at[part], hist_recv.at[slot], ctx=x
        )

    def hist_copy(src, i):
        return remote(
            src.at[i], hist.at[i], hist_send.at[i], hist_recv.at[i],
            ctx=lax.rem(me + 2, n_ctx),
        )

    def p_copy(i):
        return remote(p_out.at[i], p_in.at[i], p_send.at[i], p_recv.at[i], ctx=partner)

    def f_copy(i):
        return remote(f_out.at[i], f_in.at[i], f_send.at[i], f_recv.at[i], ctx=partner)

    def columns(c):
        return pl.ds(pl.multiple_of(c * width, 128), width)

    def out_copy(t):
        at = pl.ds(pl.multiple_of(t * sub, 128), sub)
        return remote(
            mixed.at[:, at], out_ref.at[:, at], out_send.at[t], out_recv.at[t], section=after
        )

    def chunk(n):
        row = lax.rem(z + n // parts, rows_of)
        part = lax.rem(n, parts)
        return row * parts + part, row, part

    @pl.when(me < n_ctx - 1)
    def _():
        edge_copy().start()

    msg_copy(partner_step, me).start()
    for step in range(n_ctx - 1, 0, -1):

        @pl.when(step != partner_step)
        def _():
            msg_copy(step, me).start()

    for step in range(rows_of - 1, 0, -1):
        taps_copy(step, z).start()

    @pl.when(z > 0)
    def _():
        for part in range(parts):
            tail_copy(part).start()

    def wait_msg(c):
        @pl.when(c != me)
        def _():
            msg_copy(lax.rem(me - c + n_ctx, n_ctx), c).wait_recv()

    @pl.when(me > 0)
    def _():
        edge_copy().wait_recv()
        got = edge_in[...].astype(F32)
        edges[0:6, :half] = got[0:6]
        edges[0:6, half:] = got[6:12]

    def place_edge(c):
        @pl.when(me == 0)
        def _():
            edges[0:6, columns(c)] = msgs[c].astype(F32)[9:15]

    def feature(ref, at, m, weights):
        rows = ref[:, at].astype(F32)
        ends = edges[0:6, at]
        older, newer = ends[2 * m : 2 * m + 1], ends[2 * m + 1 : 2 * m + 2]
        place = lax.broadcasted_iota(jnp.int32, rows.shape, 0)
        one = jnp.where(place == 0, newer, pltpu.roll(rows, 1, 0))
        two = jnp.where(
            place == 0, older, jnp.where(place == 1, newer, pltpu.roll(rows, 2, 0))
        )
        taps = weights[3 * m : 3 * m + 3]
        return taps[0:1] * rows + taps[1:2] * one + taps[2:3] * two

    def lanes(c, part):
        for lane in range(0, sub, 128):
            inside = pl.ds(pl.multiple_of(part * sub + lane, 128), 128)
            at = pl.ds(pl.multiple_of(c * width + part * sub + lane, 128), 128)
            yield lane, at, msgs[c, :, inside].astype(F32)

    def product(c, part, dst, slot):
        for lane, at, weights in lanes(c, part):
            key = feature(k_ref, at, 1, weights)
            value = feature(v_ref, at, 2, weights)
            dst[slot, :, lane : lane + 128] = (key * value).astype(BF16)

    def partner_products(n, carry):
        slot, row, part = chunk(n)
        c = 2 * row + 1 - x

        @pl.when(part == 0)
        def _():
            wait_msg(c)
            place_edge(c)

        product(c, part, p_out, slot)
        p_copy(slot).start()
        return carry

    lax.fori_loop(0, chunks, partner_products, 0)

    def own_products(n, carry):
        slot, row, part = chunk(n)
        c = 2 * row + x

        @pl.when(part == 0)
        def _():
            wait_msg(c)
            place_edge(c)

        product(c, part, p_own, slot)

        @pl.when((x == 1) & (z < rows_of - 1))
        def _():
            hist_copy(p_own, slot).start()

        return carry

    lax.fori_loop(0, chunks, own_products, 0)
    for load in loads[7:]:
        load.wait()
    fwd_ref[0], fwd_ref[1] = two_terms(fwd_f32[...])
    inv_ref[0], inv_ref[1] = two_terms(inv_f32[...])

    def finish(c, part, filtered):
        for lane, at, weights in lanes(c, part):
            query = feature(q_ref, at, 0, weights)
            mixed[:, at] = (query * filtered[:, lane : lane + 128]).astype(BF16)
        out_copy(c * parts + part).start()

    def from_partner(n):
        slot, row, part = chunk(n)
        f_copy(slot).wait_recv()
        finish(2 * row + 1 - x, part, f_in[slot].astype(F32))

    def spectrum(window):
        return dot(fwd_ref[0], window) + dot(fwd_ref[1], window)

    def filtered_block(current, real, imag):
        window = spectrum(jnp.concatenate([prev[...], current], axis=0))
        one, two = window[:block], window[block:]
        result = jnp.concatenate([one * real - two * imag, one * imag + two * real], axis=0)
        high, low = two_terms(result)
        return dot(inv_ref[0], high) + (dot(inv_ref[1], high) + dot(inv_ref[0], low))

    def wait_hist(slot):
        @pl.when((z > 0) | (slot >= parts))
        def _():
            hist_copy(p_own, slot).wait_recv()

    def main(n, carry):
        slot, row, part = chunk(n)

        @pl.when((n >= parts) & (part == 0))
        def _():
            taps_copy(lax.rem(z - row + rows_of, rows_of), row).wait_recv()

        at = pl.ds(pl.multiple_of(part * sub, 128), sub)
        taps = taps_all[row, at, :]
        over = (((1,), (1,)), ((), ()))
        response = lax.dot_general(
            fwd_ref[0, :, :block], taps, over, preferred_element_type=F32
        ) + lax.dot_general(fwd_ref[1, :, :block], taps, over, preferred_element_type=F32)
        gain = msgs[2 * row + x, :, at].astype(F32)[15:16]
        real, imag = response[:block] + gain, response[block:]

        p_copy(slot).wait_recv()

        @pl.when((x == 0) & (z < rows_of - 1))
        def _():
            hist_copy(p_in, slot).start()

        @pl.when(x == 0)
        def _():
            prev[...] = p_own[slot]

        @pl.when(x == 1)
        def _():
            wait_hist(slot)
            prev[...] = hist[slot]

        f_out[slot] = filtered_block(p_in[slot], real, imag).astype(BF16)
        f_copy(slot).start()

        @pl.when(x == 0)
        def _():
            wait_hist(slot)
            prev[...] = hist[slot]

        @pl.when(x == 1)
        def _():
            prev[...] = p_in[slot]

        finish(2 * row + x, part, filtered_block(p_own[slot], real, imag))

        @pl.when(n > 0)
        def _():
            from_partner(n - 1)

        return carry

    lax.fori_loop(0, chunks, main, 0)
    from_partner(chunks - 1)

    @pl.when(me < n_ctx - 1)
    def _():
        edge_copy().wait_send()

    for step in range(1, n_ctx):
        msg_copy(step, me).wait_send()
    for step in range(1, rows_of):
        taps_copy(step, z).wait_send()

    @pl.when(z > 0)
    def _():
        for part in range(parts):
            tail_copy(part).wait_send()

    def drain(i, carry):
        p_copy(i).wait_send()
        f_copy(i).wait_send()

        @pl.when(z < rows_of - 1)
        def _():
            hist_copy(p_own, i).wait_send()

        return carry

    lax.fori_loop(0, chunks, drain, 0)

    def drain_out(t, carry):
        out_copy(t).wait()
        return carry

    lax.fori_loop(0, 2 * chunks, drain_out, 0)


def body(n_section, n_ctx, query, key, value, short_taps, long_taps, skip_gain, prior_qkv, prior_product):
    block, channels = query.shape
    width = channels // n_ctx
    rows_of = n_ctx // 2
    forward, inverse = transforms(block)
    hbm = pl.BlockSpec(memory_space=pl.ANY)
    sub = min(width, CHUNK)
    chunks = rows_of * width // sub
    slots = (chunks, block, sub)
    sems = pltpu.SemaphoreType.DMA
    return pl.pallas_call(
        functools.partial(kernel, n_section, n_ctx),
        out_shape=jax.ShapeDtypeStruct(query.shape, BF16),
        in_specs=[hbm] * 10,
        out_specs=hbm,
        scratch_shapes=[
            pltpu.VMEM((block, channels), BF16),
            pltpu.VMEM((block, channels), BF16),
            pltpu.VMEM((block, channels), BF16),
            pltpu.VMEM(short_taps.shape, BF16),
            pltpu.VMEM(skip_gain.shape, BF16),
            pltpu.VMEM(prior_qkv.shape, BF16),
            pltpu.VMEM(prior_product.shape, BF16),
            pltpu.VMEM(forward.shape, F32),
            pltpu.VMEM(inverse.shape, F32),
            pltpu.VMEM((2,) + forward.shape, BF16),
            pltpu.VMEM((2,) + inverse.shape, BF16),
            pltpu.VMEM((16, width), BF16),
            pltpu.VMEM((n_ctx, 16, width), BF16),
            pltpu.VMEM((rows_of, width, block), BF16),
            pltpu.VMEM((width // sub, block, sub), BF16),
            pltpu.VMEM((16, channels // 2), BF16),
            pltpu.VMEM((16, channels // 2), BF16),
            pltpu.VMEM((8, channels), F32),
            pltpu.VMEM(slots, BF16),
            pltpu.VMEM(slots, BF16),
            pltpu.VMEM(slots, BF16),
            pltpu.VMEM(slots, BF16),
            pltpu.VMEM((block, sub), BF16),
            pltpu.VMEM(slots, BF16),
            pltpu.VMEM(slots, BF16),
            pltpu.VMEM((block, channels), BF16),
            sems((10,)),
            sems((n_ctx,)),
            sems((n_ctx,)),
            sems((rows_of,)),
            sems((rows_of,)),
            sems((width // sub,)),
            sems((chunks,)),
            sems((chunks,)),
            sems,
            sems,
            sems((chunks,)),
            sems((chunks,)),
            sems((chunks,)),
            sems((chunks,)),
            sems((2 * chunks,)),
            sems((2 * chunks,)),
        ],
        compiler_params=pltpu.CompilerParams(
            collective_id=0, has_side_effects=True, vmem_limit_bytes=VMEM_BYTES
        ),
        cost_estimate=pl.CostEstimate(
            flops=2 * 2 * 256 * 256 * 4096, bytes_accessed=6 * 2**20, transcendentals=0
        ),
        name="paired_filter",
    )(
        query, key, value, short_taps, long_taps, skip_gain, prior_qkv, prior_product,
        jnp.asarray(forward), jnp.asarray(inverse),
    )


def solution(mesh):
    in_specs = (
        P(("section", "ctx"), None),
        P(("section", "ctx"), None),
        P(("section", "ctx"), None),
        P("section", None, None, "ctx"),
        P("section", "ctx", None),
        P("section", "ctx"),
        P("section", None, None, "ctx"),
        P("section", None, "ctx"),
    )
    out_specs = P(("section", "ctx"), None)
    run = functools.partial(body, mesh.shape["section"], mesh.shape["ctx"])
    return jax.shard_map(run, mesh=mesh, in_specs=in_specs, out_specs=out_specs, check_vma=False)
```

```python
import functools

import jax
import jax.numpy as jnp
import numpy as np
from jax import lax
from jax.experimental import pallas as pl
from jax.experimental.pallas import tpu as pltpu
from jax.sharding import PartitionSpec as P

MESH = pl.DeviceIdType.MESH
F32 = jnp.float32
BF16 = jnp.bfloat16
CHUNK = 512
VMEM_BYTES = 40 * 1024 * 1024


def transforms(block):
    size = 2 * block
    freq = (2 * np.arange(block)[:, None] + 1).astype(np.int64)
    turn = np.pi * ((freq * np.arange(size)[None, :]) % (2 * size)) / size
    forward = np.concatenate([np.cos(turn), -np.sin(turn)], axis=0)
    inverse = (forward * (2.0 / size)).T[block:]

    return forward.astype(np.float32), inverse.astype(np.float32)


def two_terms(matrix):
    high = matrix.astype(BF16)
    return high, (matrix - high.astype(F32)).astype(BF16)


def dot(a, b):
    return jnp.dot(a, b, preferred_element_type=F32)


def kernel(
    n_section, n_ctx,
    q_hbm, k_hbm, v_hbm, short_hbm, taps_hbm, gain_hbm, prior_hbm, tail_hbm, fwd_hbm, inv_hbm,
    out_ref,
    q_ref, k_ref, v_ref, short_ref, gain_ref, prior_ref, tail_ref, fwd_f32, inv_f32, fwd_ref, inv_ref, own_msg, msgs, taps_all, own_tail, edge_out, edge_in, edges,
    p_out, p_own, p_in, hist, responses, f_out, f_in, mixed,
    load_sem, msg_send, msg_recv, taps_send, taps_recv, tail_send, hist_send, hist_recv,
    edge_send, edge_recv, p_send, p_recv, f_send, f_recv, out_send, out_recv,
):
    section = lax.axis_index("section")
    me = lax.axis_index("ctx")
    rows_of = n_ctx // 2
    z, x = me // 2, me % 2
    partner = me + 1 - 2 * x
    after = lax.rem(section + 1, n_section)
    before = lax.rem(section + n_section - 1, n_section)
    block, channels = q_ref.shape
    width = channels // n_ctx
    half = channels // 2

    sub = p_out.shape[2]
    parts = width // sub

    loads = [
        pltpu.make_async_copy(src, dst, load_sem.at[i])
        for i, (src, dst) in enumerate(
            (
                (short_hbm, short_ref), (prior_hbm, prior_ref), (gain_hbm, gain_ref),
                (tail_hbm, tail_ref), (k_hbm, k_ref), (v_hbm, v_ref), (q_hbm, q_ref),
                (taps_hbm.at[0], taps_all.at[z]), (fwd_hbm, fwd_f32), (inv_hbm, inv_f32),
            )
        )
    ]
    for load in loads:
        load.start()

    barrier = pltpu.get_barrier_semaphore()
    for step in range(1, n_ctx):
        pl.semaphore_signal(
            barrier, inc=1, device_id={"ctx": lax.rem(me + step, n_ctx)}, device_id_type=MESH
        )
    for other in (after, before):
        pl.semaphore_signal(barrier, inc=1, device_id={"section": other}, device_id_type=MESH)

    for load in loads[:4]:
        load.wait()
    pieces = [short_ref[0, m].astype(F32) for m in range(3)]
    pieces += [prior_ref[0, m].astype(F32) for m in range(3)]
    pieces.append(gain_ref[...].astype(F32))
    own_msg[...] = jnp.concatenate(pieces, axis=0).astype(BF16)
    msgs[me] = own_msg[...]
    tail = jnp.concatenate(
        [jnp.zeros((1, width), F32), tail_ref[0].astype(F32)], axis=0
    ).astype(BF16)
    for part in range(parts):
        own_tail[part] = tail[:, part * sub : (part + 1) * sub]

    @pl.when(z == 0)
    def _():
        for part in range(parts):
            hist[part] = own_tail[part]

    for load in loads[4:7]:
        load.wait()
    last = [ref[block - 16:, :].astype(F32)[14:] for ref in (q_ref, k_ref, v_ref)]
    edge_out[...] = jnp.concatenate(
        [piece[:, :half] for piece in last]
        + [piece[:, half:] for piece in last]
        + [jnp.zeros((4, half), F32)],
        axis=0,
    ).astype(BF16)

    pl.semaphore_wait(barrier, n_ctx + 1)

    def remote(src, dst, send, recv, **where):
        return pltpu.make_async_remote_copy(
            src_ref=src, dst_ref=dst, send_sem=send, recv_sem=recv,
            device_id=where, device_id_type=MESH,
        )

    chunks = rows_of * parts
    partner_step = lax.rem(partner - me + n_ctx, n_ctx)

    def edge_copy():
        return remote(edge_out, edge_in, edge_send, edge_recv, ctx=lax.rem(me + 1, n_ctx))

    def msg_copy(step, slot):
        return remote(
            own_msg, msgs.at[slot], msg_send.at[step], msg_recv.at[step],
            ctx=lax.rem(me + step, n_ctx),
        )

    def taps_copy(step, slot):
        return remote(
            taps_hbm.at[0], taps_all.at[slot], taps_send.at[step], taps_recv.at[step],
            ctx=lax.rem(z + step, rows_of) * 2 + x,
        )

    def tail_copy(part):
        slot = z * parts + part
        return remote(
            own_tail.at[part], hist.at[slot], tail_send.at[part], hist_recv.at[slot], ctx=x
        )

    def hist_copy(src, i):
        return remote(
            src.at[i], hist.at[i], hist_send.at[i], hist_recv.at[i],
            ctx=lax.rem(me + 2, n_ctx),
        )

    def p_copy(i):
        return remote(p_out.at[i], p_in.at[i], p_send.at[i], p_recv.at[i], ctx=partner)

    def f_copy(i):
        return remote(f_out.at[i], f_in.at[i], f_send.at[i], f_recv.at[i], ctx=partner)

    def columns(c):
        return pl.ds(pl.multiple_of(c * width, 128), width)

    def out_copy(t):
        at = pl.ds(pl.multiple_of(t * sub, 128), sub)
        return remote(
            mixed.at[:, at], out_ref.at[:, at], out_send.at[t], out_recv.at[t], section=after
        )

    def chunk(n):
        row = lax.rem(z + n // parts, rows_of)
        part = lax.rem(n, parts)
        return row * parts + part, row, part

    @pl.when(me < n_ctx - 1)
    def _():
        edge_copy().start()

    msg_copy(partner_step, me).start()
    for step in range(n_ctx - 1, 0, -1):

        @pl.when(step != partner_step)
        def _():
            msg_copy(step, me).start()

    for step in range(rows_of - 1, 0, -1):
        taps_copy(step, z).start()

    @pl.when(z > 0)
    def _():
        for part in range(parts):
            tail_copy(part).start()

    def wait_msg(c):
        @pl.when(c != me)
        def _():
            msg_copy(lax.rem(me - c + n_ctx, n_ctx), c).wait_recv()

    @pl.when(me > 0)
    def _():
        edge_copy().wait_recv()
        got = edge_in[...].astype(F32)
        edges[0:6, :half] = got[0:6]
        edges[0:6, half:] = got[6:12]

    def place_edge(c):
        @pl.when(me == 0)
        def _():
            edges[0:6, columns(c)] = msgs[c].astype(F32)[9:15]

    def feature(ref, at, m, weights):
        rows = ref[:, at].astype(F32)
        ends = edges[0:6, at]
        older, newer = ends[2 * m : 2 * m + 1], ends[2 * m + 1 : 2 * m + 2]
        place = lax.broadcasted_iota(jnp.int32, rows.shape, 0)
        one = jnp.where(place == 0, newer, pltpu.roll(rows, 1, 0))
        two = jnp.where(
            place == 0, older, jnp.where(place == 1, newer, pltpu.roll(rows, 2, 0))
        )
        taps = weights[3 * m : 3 * m + 3]
        return taps[0:1] * rows + taps[1:2] * one + taps[2:3] * two

    def lanes(c, part):
        for lane in range(0, sub, 128):
            inside = pl.ds(pl.multiple_of(part * sub + lane, 128), 128)
            at = pl.ds(pl.multiple_of(c * width + part * sub + lane, 128), 128)
            yield lane, at, msgs[c, :, inside].astype(F32)

    def product(c, part, dst, slot):
        for lane, at, weights in lanes(c, part):
            key = feature(k_ref, at, 1, weights)
            value = feature(v_ref, at, 2, weights)
            dst[slot, :, lane : lane + 128] = (key * value).astype(BF16)

    def partner_products(n, carry):
        slot, row, part = chunk(n)
        c = 2 * row + 1 - x

        @pl.when(part == 0)
        def _():
            wait_msg(c)
            place_edge(c)

        product(c, part, p_out, slot)
        p_copy(slot).start()
        return carry

    lax.fori_loop(0, chunks, partner_products, 0)

    def own_products(n, carry):
        slot, row, part = chunk(n + parts)
        c = 2 * row + x

        @pl.when(part == 0)
        def _():
            wait_msg(c)
            place_edge(c)

        product(c, part, p_own, slot)

        @pl.when((x == 1) & (z < rows_of - 1))
        def _():
            hist_copy(p_own, slot).start()

        return carry

    lax.fori_loop(0, chunks, own_products, 0)
    for load in loads[7:]:
        load.wait()
    fwd_ref[0], fwd_ref[1] = two_terms(fwd_f32[...])
    inv_ref[0], inv_ref[1] = two_terms(inv_f32[...])

    def finish(c, part, filtered):
        for lane, at, weights in lanes(c, part):
            query = feature(q_ref, at, 0, weights)
            mixed[:, at] = (query * filtered[:, lane : lane + 128]).astype(BF16)
        out_copy(c * parts + part).start()

    def from_partner(n):
        slot, row, part = chunk(n)
        f_copy(slot).wait_recv()
        finish(2 * row + 1 - x, part, f_in[slot].astype(F32))

    def spectrum(window):
        return dot(fwd_ref[0], window) + dot(fwd_ref[1], window)

    def filtered_block(slot, before_ref, current_ref):
        window = jnp.concatenate([before_ref[slot], current_ref[slot]], axis=0)
        waves = spectrum(window)
        one, two = waves[:block], waves[block:]
        real, imag = responses[slot, :block], responses[slot, block:]
        result = jnp.concatenate([one * real - two * imag, one * imag + two * real], axis=0)
        high, low = two_terms(result)
        return dot(inv_ref[0], high) + (dot(inv_ref[1], high) + dot(inv_ref[0], low))

    def give_back(slot, before_ref):
        f_out[slot] = filtered_block(slot, before_ref, p_in).astype(BF16)
        f_copy(slot).start()

    def keep(n, before_ref):
        slot, row, part = chunk(n)
        finish(2 * row + x, part, filtered_block(slot, before_ref, p_own))

    def wait_hist(slot):
        @pl.when((z > 0) | (slot >= parts))
        def _():
            hist_copy(p_own, slot).wait_recv()

    def respond(n):
        slot, row, part = chunk(n)

        @pl.when((n >= parts) & (part == 0))
        def _():
            taps_copy(lax.rem(z - row + rows_of, rows_of), row).wait_recv()

        at = pl.ds(pl.multiple_of(part * sub, 128), sub)
        taps = taps_all[row, at, :]
        over = (((1,), (1,)), ((), ()))
        response = lax.dot_general(
            fwd_ref[0, :, :block], taps, over, preferred_element_type=F32
        ) + lax.dot_general(fwd_ref[1, :, :block], taps, over, preferred_element_type=F32)
        gain = msgs[2 * row + x, :, at].astype(F32)[15:16]
        responses[slot, :block] = response[:block] + gain
        responses[slot, block:] = response[block:]

    def with_product(n, carry):
        slot, _, _ = chunk(n)
        p_copy(slot).wait_recv()

        @pl.when((x == 0) & (z < rows_of - 1))
        def _():
            hist_copy(p_in, slot).start()

        respond(n)

        @pl.when(x == 0)
        def _():
            give_back(slot, p_own)

        @pl.when(x == 1)
        def _():
            keep(n, p_in)

        return carry

    def with_history(n, carry):
        slot, _, _ = chunk(n)
        wait_hist(slot)

        @pl.when(x == 0)
        def _():
            keep(n, hist)

        @pl.when(x == 1)
        def _():
            give_back(slot, hist)

        return carry

    def with_partner(n, carry):
        from_partner(n)
        return carry

    lax.fori_loop(0, chunks, with_product, 0)
    lax.fori_loop(0, chunks, with_history, 0)
    lax.fori_loop(0, chunks, with_partner, 0)

    @pl.when(me < n_ctx - 1)
    def _():
        edge_copy().wait_send()

    for step in range(1, n_ctx):
        msg_copy(step, me).wait_send()
    for step in range(1, rows_of):
        taps_copy(step, z).wait_send()

    @pl.when(z > 0)
    def _():
        for part in range(parts):
            tail_copy(part).wait_send()

    def drain(i, carry):
        p_copy(i).wait_send()
        f_copy(i).wait_send()

        @pl.when(z < rows_of - 1)
        def _():
            hist_copy(p_own, i).wait_send()

        return carry

    lax.fori_loop(0, chunks, drain, 0)

    def drain_out(t, carry):
        out_copy(t).wait()
        return carry

    lax.fori_loop(0, 2 * chunks, drain_out, 0)


def body(n_section, n_ctx, query, key, value, short_taps, long_taps, skip_gain, prior_qkv, prior_product):
    block, channels = query.shape
    width = channels // n_ctx
    rows_of = n_ctx // 2
    forward, inverse = transforms(block)
    hbm = pl.BlockSpec(memory_space=pltpu.HBM)
    sub = min(width, CHUNK)
    chunks = rows_of * width // sub
    slots = (chunks, block, sub)
    sems = pltpu.SemaphoreType.DMA
    return pl.pallas_call(
        functools.partial(kernel, n_section, n_ctx),
        out_shape=jax.ShapeDtypeStruct(query.shape, BF16),
        in_specs=[hbm] * 10,
        out_specs=pl.BlockSpec(memory_space=pl.ANY),
        scratch_shapes=[
            pltpu.VMEM((block, channels), BF16),
            pltpu.VMEM((block, channels), BF16),
            pltpu.VMEM((block, channels), BF16),
            pltpu.VMEM(short_taps.shape, BF16),
            pltpu.VMEM(skip_gain.shape, BF16),
            pltpu.VMEM(prior_qkv.shape, BF16),
            pltpu.VMEM(prior_product.shape, BF16),
            pltpu.VMEM(forward.shape, F32),
            pltpu.VMEM(inverse.shape, F32),
            pltpu.VMEM((2,) + forward.shape, BF16),
            pltpu.VMEM((2,) + inverse.shape, BF16),
            pltpu.VMEM((16, width), BF16),
            pltpu.VMEM((n_ctx, 16, width), BF16),
            pltpu.VMEM((rows_of, width, block), BF16),
            pltpu.VMEM((width // sub, block, sub), BF16),
            pltpu.VMEM((16, channels // 2), BF16),
            pltpu.VMEM((16, channels // 2), BF16),
            pltpu.VMEM((8, channels), F32),
            pltpu.VMEM(slots, BF16),
            pltpu.VMEM(slots, BF16),
            pltpu.VMEM(slots, BF16),
            pltpu.VMEM(slots, BF16),
            pltpu.VMEM((chunks, 2 * block, sub), F32),
            pltpu.VMEM(slots, BF16),
            pltpu.VMEM(slots, BF16),
            pltpu.VMEM((block, channels), BF16),
            sems((10,)),
            sems((n_ctx,)),
            sems((n_ctx,)),
            sems((rows_of,)),
            sems((rows_of,)),
            sems((width // sub,)),
            sems((chunks,)),
            sems((chunks,)),
            sems,
            sems,
            sems((chunks,)),
            sems((chunks,)),
            sems((chunks,)),
            sems((chunks,)),
            sems((2 * chunks,)),
            sems((2 * chunks,)),
        ],
        compiler_params=pltpu.CompilerParams(
            collective_id=0, has_side_effects=True, vmem_limit_bytes=VMEM_BYTES
        ),
        cost_estimate=pl.CostEstimate(
            flops=2 * 2 * 256 * 256 * 4096, bytes_accessed=6 * 2**20, transcendentals=0
        ),
        name="paired_filter",
    )(
        query, key, value, short_taps, long_taps, skip_gain, prior_qkv, prior_product,
        jnp.asarray(forward), jnp.asarray(inverse),
    )


def solution(mesh):
    in_specs = (
        P(("section", "ctx"), None),
        P(("section", "ctx"), None),
        P(("section", "ctx"), None),
        P("section", None, None, "ctx"),
        P("section", "ctx", None),
        P("section", "ctx"),
        P("section", None, None, "ctx"),
        P("section", None, "ctx"),
    )
    out_specs = P(("section", "ctx"), None)
    run = functools.partial(body, mesh.shape["section"], mesh.shape["ctx"])
    return jax.shard_map(run, mesh=mesh, in_specs=in_specs, out_specs=out_specs, check_vma=False)
```

```python
import functools

import jax
import jax.numpy as jnp
import numpy as np
from jax import lax
from jax.experimental import pallas as pl
from jax.experimental.pallas import tpu as pltpu
from jax.sharding import PartitionSpec as P

MESH = pl.DeviceIdType.MESH
F32 = jnp.float32
BF16 = jnp.bfloat16
CHUNK = 512
VMEM_BYTES = 64 * 1024 * 1024


def transforms(block):
    size = 2 * block
    freq = (2 * np.arange(block)[:, None] + 1).astype(np.int64)
    turn = np.pi * ((freq * np.arange(size)[None, :]) % (2 * size)) / size
    forward = np.concatenate([np.cos(turn), -np.sin(turn)], axis=0)
    inverse = (forward * (2.0 / size)).T[block:]

    return forward.astype(np.float32), inverse.astype(np.float32)


def two_terms(matrix):
    high = matrix.astype(BF16)
    return high, (matrix - high.astype(F32)).astype(BF16)


def dot(a, b):
    return jnp.dot(a, b, preferred_element_type=F32)


def kernel(
    n_section, n_ctx,
    q_hbm, k_hbm, v_hbm, short_hbm, taps_hbm, gain_hbm, prior_hbm, tail_hbm, fwd_hbm, inv_hbm,
    out_ref,
    q_ref, k_ref, v_ref, short_ref, gain_ref, prior_ref, tail_ref, fwd_f32, inv_f32, fwd_ref, inv_ref, own_msg, msgs, taps_all, own_tail, edge_out, edge_in, edges,
    p_out, p_own, p_in, hist, responses, f_out, f_in, mixed,
    load_sem, msg_send, msg_recv, taps_send, taps_recv, tail_send, hist_send, hist_recv,
    edge_send, edge_recv, p_send, p_recv, f_send, f_recv, out_send, out_recv,
):
    section = lax.axis_index("section")
    me = lax.axis_index("ctx")
    rows_of = n_ctx // 2
    z, x = me // 2, me % 2
    partner = me + 1 - 2 * x
    after = lax.rem(section + 1, n_section)
    before = lax.rem(section + n_section - 1, n_section)
    block, channels = q_ref.shape
    width = channels // n_ctx
    half = channels // 2

    sub = p_out.shape[2]
    parts = width // sub

    loads = [
        pltpu.make_async_copy(src, dst, load_sem.at[i])
        for i, (src, dst) in enumerate(
            (
                (short_hbm, short_ref), (prior_hbm, prior_ref), (gain_hbm, gain_ref),
                (tail_hbm, tail_ref), (k_hbm, k_ref), (v_hbm, v_ref), (q_hbm, q_ref),
                (taps_hbm.at[0], taps_all.at[z]), (fwd_hbm, fwd_f32), (inv_hbm, inv_f32),
            )
        )
    ]
    for load in loads:
        load.start()

    barrier = pltpu.get_barrier_semaphore()
    for step in range(1, n_ctx):
        pl.semaphore_signal(
            barrier, inc=1, device_id={"ctx": lax.rem(me + step, n_ctx)}, device_id_type=MESH
        )
    for other in (after, before):
        pl.semaphore_signal(barrier, inc=1, device_id={"section": other}, device_id_type=MESH)

    for load in loads[:4]:
        load.wait()
    pieces = [short_ref[0, m].astype(F32) for m in range(3)]
    pieces += [prior_ref[0, m].astype(F32) for m in range(3)]
    pieces.append(gain_ref[...].astype(F32))
    own_msg[...] = jnp.concatenate(pieces, axis=0).astype(BF16)
    msgs[me] = own_msg[...]
    tail = jnp.concatenate(
        [jnp.zeros((1, width), F32), tail_ref[0].astype(F32)], axis=0
    ).astype(BF16)
    for part in range(parts):
        own_tail[part] = tail[:, part * sub : (part + 1) * sub]

    @pl.when(z == 0)
    def _():
        for part in range(parts):
            hist[part] = own_tail[part]

    for load in loads[4:7]:
        load.wait()
    last = [ref[block - 16:, :].astype(F32)[14:] for ref in (q_ref, k_ref, v_ref)]
    edge_out[...] = jnp.concatenate(
        [piece[:, :half] for piece in last]
        + [piece[:, half:] for piece in last]
        + [jnp.zeros((4, half), F32)],
        axis=0,
    ).astype(BF16)

    pl.semaphore_wait(barrier, n_ctx + 1)

    def remote(src, dst, send, recv, **where):
        return pltpu.make_async_remote_copy(
            src_ref=src, dst_ref=dst, send_sem=send, recv_sem=recv,
            device_id=where, device_id_type=MESH,
        )

    chunks = rows_of * parts
    partner_step = lax.rem(partner - me + n_ctx, n_ctx)

    def edge_copy():
        return remote(edge_out, edge_in, edge_send, edge_recv, ctx=lax.rem(me + 1, n_ctx))

    def msg_copy(step, slot):
        return remote(
            own_msg, msgs.at[slot], msg_send.at[step], msg_recv.at[step],
            ctx=lax.rem(me + step, n_ctx),
        )

    def taps_copy(src, owner, up):
        return remote(
            src, taps_all.at[owner], taps_send.at[int(up), owner], taps_recv.at[owner],
            ctx=lax.rem(me + (2 if up else n_ctx - 2), n_ctx),
        )

    def tail_copy(part):
        slot = z * parts + part
        return remote(
            own_tail.at[part], hist.at[slot], tail_send.at[part], hist_recv.at[slot], ctx=x
        )

    def hist_copy(src, i):
        return remote(
            src.at[i], hist.at[i], hist_send.at[i], hist_recv.at[i],
            ctx=lax.rem(me + 2, n_ctx),
        )

    def p_copy(i):
        return remote(p_out.at[i], p_in.at[i], p_send.at[i], p_recv.at[i], ctx=partner)

    def f_copy(i):
        return remote(f_out.at[i], f_in.at[i], f_send.at[i], f_recv.at[i], ctx=partner)

    def columns(c):
        return pl.ds(pl.multiple_of(c * width, 128), width)

    def out_copy(t):
        at = pl.ds(pl.multiple_of(t * sub, 128), sub)
        return remote(
            mixed.at[:, at], out_ref.at[:, at], out_send.at[t], out_recv.at[t], section=after
        )

    def chunk(n, at=z):
        step = n // parts
        row = jnp.where(step < rows_of - at, at + step, rows_of - 1 - step)
        part = lax.rem(n, parts)
        return row * parts + part, row, part

    @pl.when(me < n_ctx - 1)
    def _():
        edge_copy().start()

    msg_copy(partner_step, me).start()
    for step in range(n_ctx - 1, 0, -1):

        @pl.when(step != partner_step)
        def _():
            msg_copy(step, me).start()

    @pl.when(z < rows_of - 1)
    def _():
        taps_copy(taps_hbm.at[0], z, True).start()

    @pl.when(z > 0)
    def _():
        taps_copy(taps_hbm.at[0], z, False).start()

    @pl.when(z > 0)
    def _():
        for part in range(parts):
            tail_copy(part).start()

    def wait_msg(c):
        @pl.when(c != me)
        def _():
            msg_copy(lax.rem(me - c + n_ctx, n_ctx), c).wait_recv()

    @pl.when(me > 0)
    def _():
        edge_copy().wait_recv()
        got = edge_in[...].astype(F32)
        edges[0:6, :half] = got[0:6]
        edges[0:6, half:] = got[6:12]

    def place_edge(c):
        @pl.when(me == 0)
        def _():
            edges[0:6, columns(c)] = msgs[c].astype(F32)[9:15]

    def feature(ref, at, m, weights):
        rows = ref[:, at].astype(F32)
        ends = edges[0:6, at]
        older, newer = ends[2 * m : 2 * m + 1], ends[2 * m + 1 : 2 * m + 2]
        place = lax.broadcasted_iota(jnp.int32, rows.shape, 0)
        one = jnp.where(place == 0, newer, pltpu.roll(rows, 1, 0))
        two = jnp.where(
            place == 0, older, jnp.where(place == 1, newer, pltpu.roll(rows, 2, 0))
        )
        taps = weights[3 * m : 3 * m + 3]
        return taps[0:1] * rows + taps[1:2] * one + taps[2:3] * two

    def lanes(c, part):
        for lane in range(0, sub, 128):
            inside = pl.ds(pl.multiple_of(part * sub + lane, 128), 128)
            at = pl.ds(pl.multiple_of(c * width + part * sub + lane, 128), 128)
            yield lane, at, msgs[c, :, inside].astype(F32)

    def product(c, part, dst, slot):
        for lane, at, weights in lanes(c, part):
            key = feature(k_ref, at, 1, weights)
            value = feature(v_ref, at, 2, weights)
            dst[slot, :, lane : lane + 128] = (key * value).astype(BF16)

    def partner_products(n, carry):
        slot, row, part = chunk(n)
        c = 2 * row + 1 - x

        @pl.when(part == 0)
        def _():
            wait_msg(c)
            place_edge(c)

        product(c, part, p_out, slot)
        p_copy(slot).start()
        return carry

    lax.fori_loop(0, chunks, partner_products, 0)

    def own_products(n, carry):
        slot, row, part = chunk(n, jnp.minimum(z + 1, rows_of - 1))
        c = 2 * row + x

        @pl.when(part == 0)
        def _():
            wait_msg(c)
            place_edge(c)

        product(c, part, p_own, slot)

        @pl.when((x == 1) & (z < rows_of - 1))
        def _():
            hist_copy(p_own, slot).start()

        return carry

    lax.fori_loop(0, chunks, own_products, 0)
    for load in loads[7:]:
        load.wait()
    fwd_ref[0], fwd_ref[1] = two_terms(fwd_f32[...])
    inv_ref[0], inv_ref[1] = two_terms(inv_f32[...])

    def finish(c, part, filtered):
        for lane, at, weights in lanes(c, part):
            query = feature(q_ref, at, 0, weights)
            mixed[:, at] = (query * filtered[:, lane : lane + 128]).astype(BF16)
        out_copy(c * parts + part).start()

    def from_partner(n):
        slot, row, part = chunk(n)
        f_copy(slot).wait_recv()
        finish(2 * row + 1 - x, part, f_in[slot].astype(F32))

    def spectrum(window):
        return dot(fwd_ref[0], window) + dot(fwd_ref[1], window)

    def filtered_block(slot, before_ref, current_ref):
        window = jnp.concatenate([before_ref[slot], current_ref[slot]], axis=0)
        waves = spectrum(window)
        one, two = waves[:block], waves[block:]
        real, imag = responses[slot, :block], responses[slot, block:]
        result = jnp.concatenate([one * real - two * imag, one * imag + two * real], axis=0)
        high, low = two_terms(result)
        return dot(inv_ref[0], high) + (dot(inv_ref[1], high) + dot(inv_ref[0], low))

    def give_back(slot, before_ref):
        f_out[slot] = filtered_block(slot, before_ref, p_in).astype(BF16)
        f_copy(slot).start()

    def keep(n, before_ref):
        slot, row, part = chunk(n)
        finish(2 * row + x, part, filtered_block(slot, before_ref, p_own))

    def wait_hist(slot):
        @pl.when((z > 0) | (slot >= parts))
        def _():
            hist_copy(p_own, slot).wait_recv()

    def relay(step):
        below, above = z - step, z + step

        @pl.when(below >= 0)
        def _():
            taps_copy(taps_all.at[below], below, True).wait_recv()

            @pl.when(z < rows_of - 1)
            def _():
                taps_copy(taps_all.at[below], below, True).start()

        @pl.when(above < rows_of)
        def _():
            taps_copy(taps_all.at[above], above, False).wait_recv()

            @pl.when(z > 0)
            def _():
                taps_copy(taps_all.at[above], above, False).start()

    def respond(n):
        slot, row, part = chunk(n)
        at = pl.ds(pl.multiple_of(part * sub, 128), sub)
        taps = taps_all[row, at, :]
        over = (((1,), (1,)), ((), ()))
        response = lax.dot_general(
            fwd_ref[0, :, :block], taps, over, preferred_element_type=F32
        ) + lax.dot_general(fwd_ref[1, :, :block], taps, over, preferred_element_type=F32)
        gain = msgs[2 * row + x, :, at].astype(F32)[15:16]
        responses[slot, :block] = response[:block] + gain
        responses[slot, block:] = response[block:]

    def with_product(n, carry):
        slot, _, part = chunk(n)
        p_copy(slot).wait_recv()

        @pl.when((x == 0) & (z < rows_of - 1))
        def _():
            hist_copy(p_in, slot).start()

        @pl.when((n >= parts) & (part == 0))
        def _():
            relay(n // parts)

        respond(n)

        @pl.when(x == 0)
        def _():
            give_back(slot, p_own)

        @pl.when((x == 1) & (n > 0))
        def _():
            with_history(n - 1)

        return carry

    def with_history(n):
        slot, _, _ = chunk(n)
        wait_hist(slot)
        give_back(slot, hist)

    def own_rows(n, carry):
        slot, _, _ = chunk(n)

        @pl.when(x == 0)
        def _():
            wait_hist(slot)
            keep(n, hist)

        @pl.when(x == 1)
        def _():
            keep(n, p_in)

        return carry

    def with_partner(n, carry):
        from_partner(n)
        return carry

    lax.fori_loop(0, chunks, with_product, 0)

    @pl.when(x == 1)
    def _():
        with_history(chunks - 1)

    lax.fori_loop(0, chunks, own_rows, 0)
    lax.fori_loop(0, chunks, with_partner, 0)

    @pl.when(me < n_ctx - 1)
    def _():
        edge_copy().wait_send()

    for step in range(1, n_ctx):
        msg_copy(step, me).wait_send()

    def drain_taps(owner, carry):
        @pl.when((owner <= z) & (z < rows_of - 1))
        def _():
            taps_copy(taps_all.at[owner], owner, True).wait_send()

        @pl.when((owner >= z) & (z > 0))
        def _():
            taps_copy(taps_all.at[owner], owner, False).wait_send()

        return carry

    lax.fori_loop(0, rows_of, drain_taps, 0)

    @pl.when(z > 0)
    def _():
        for part in range(parts):
            tail_copy(part).wait_send()

    def drain(i, carry):
        p_copy(i).wait_send()
        f_copy(i).wait_send()

        @pl.when(z < rows_of - 1)
        def _():
            hist_copy(p_own, i).wait_send()

        return carry

    lax.fori_loop(0, chunks, drain, 0)

    def drain_out(t, carry):
        out_copy(t).wait()
        return carry

    lax.fori_loop(0, 2 * chunks, drain_out, 0)


def body(n_section, n_ctx, query, key, value, short_taps, long_taps, skip_gain, prior_qkv, prior_product):
    block, channels = query.shape
    width = channels // n_ctx
    rows_of = n_ctx // 2
    forward, inverse = transforms(block)
    hbm = pl.BlockSpec(memory_space=pltpu.HBM)
    sub = min(width, CHUNK)
    chunks = rows_of * width // sub
    slots = (chunks, block, sub)
    sems = pltpu.SemaphoreType.DMA
    return pl.pallas_call(
        functools.partial(kernel, n_section, n_ctx),
        out_shape=jax.ShapeDtypeStruct(query.shape, BF16),
        in_specs=[hbm] * 10,
        out_specs=pl.BlockSpec(memory_space=pl.ANY),
        scratch_shapes=[
            pltpu.VMEM((block, channels), BF16),
            pltpu.VMEM((block, channels), BF16),
            pltpu.VMEM((block, channels), BF16),
            pltpu.VMEM(short_taps.shape, BF16),
            pltpu.VMEM(skip_gain.shape, BF16),
            pltpu.VMEM(prior_qkv.shape, BF16),
            pltpu.VMEM(prior_product.shape, BF16),
            pltpu.VMEM(forward.shape, F32),
            pltpu.VMEM(inverse.shape, F32),
            pltpu.VMEM((2,) + forward.shape, BF16),
            pltpu.VMEM((2,) + inverse.shape, BF16),
            pltpu.VMEM((16, width), BF16),
            pltpu.VMEM((n_ctx, 16, width), BF16),
            pltpu.VMEM((rows_of, width, block), BF16),
            pltpu.VMEM((width // sub, block, sub), BF16),
            pltpu.VMEM((16, channels // 2), BF16),
            pltpu.VMEM((16, channels // 2), BF16),
            pltpu.VMEM((8, channels), F32),
            pltpu.VMEM(slots, BF16),
            pltpu.VMEM(slots, BF16),
            pltpu.VMEM(slots, BF16),
            pltpu.VMEM(slots, BF16),
            pltpu.VMEM((chunks, 2 * block, sub), F32),
            pltpu.VMEM(slots, BF16),
            pltpu.VMEM(slots, BF16),
            pltpu.VMEM((block, channels), BF16),
            sems((10,)),
            sems((n_ctx,)),
            sems((n_ctx,)),
            sems((2, rows_of)),
            sems((rows_of,)),
            sems((width // sub,)),
            sems((chunks,)),
            sems((chunks,)),
            sems,
            sems,
            sems((chunks,)),
            sems((chunks,)),
            sems((chunks,)),
            sems((chunks,)),
            sems((2 * chunks,)),
            sems((2 * chunks,)),
        ],
        compiler_params=pltpu.CompilerParams(
            collective_id=0, has_side_effects=True, vmem_limit_bytes=VMEM_BYTES
        ),
        cost_estimate=pl.CostEstimate(
            flops=2 * 2 * 256 * 256 * 4096, bytes_accessed=6 * 2**20, transcendentals=0
        ),
        name="paired_filter",
    )(
        query, key, value, short_taps, long_taps, skip_gain, prior_qkv, prior_product,
        jnp.asarray(forward), jnp.asarray(inverse),
    )


def solution(mesh):
    in_specs = (
        P(("section", "ctx"), None),
        P(("section", "ctx"), None),
        P(("section", "ctx"), None),
        P("section", None, None, "ctx"),
        P("section", "ctx", None),
        P("section", "ctx"),
        P("section", None, None, "ctx"),
        P("section", None, "ctx"),
    )
    out_specs = P(("section", "ctx"), None)
    run = functools.partial(body, mesh.shape["section"], mesh.shape["ctx"])
    return jax.shard_map(run, mesh=mesh, in_specs=in_specs, out_specs=out_specs, check_vma=False)
```

```python
import functools

import jax
import jax.numpy as jnp
import numpy as np
from jax import lax
from jax.experimental import pallas as pl
from jax.experimental.pallas import tpu as pltpu
from jax.sharding import PartitionSpec as P

MESH = pl.DeviceIdType.MESH
F32 = jnp.float32
BF16 = jnp.bfloat16
CHUNK = 256
VMEM_BYTES = 64 * 1024 * 1024


def transforms(block):
    size = 2 * block
    freq = (2 * np.arange(block)[:, None] + 1).astype(np.int64)
    turn = np.pi * ((freq * np.arange(size)[None, :]) % (2 * size)) / size
    forward = np.concatenate([np.cos(turn), -np.sin(turn)], axis=0)
    inverse = (forward * (2.0 / size)).T[block:]

    return forward.astype(np.float32), inverse.astype(np.float32)


def two_terms(matrix):
    high = matrix.astype(BF16)
    return high, (matrix - high.astype(F32)).astype(BF16)


def dot(a, b):
    return jnp.dot(a, b, preferred_element_type=F32)


def kernel(
    n_section, n_ctx,
    q_hbm, k_hbm, v_hbm, short_hbm, taps_hbm, gain_hbm, prior_hbm, tail_hbm, fwd_hbm, inv_hbm,
    out_ref,
    q_ref, k_ref, v_ref, short_ref, gain_ref, prior_ref, tail_ref, fwd_f32, inv_f32, fwd_ref, inv_ref, own_msg, msgs, taps_all, own_tail, edge_out, edge_in, edges,
    p_out, p_own, p_in, hist, responses, f_out, f_in, mixed,
    load_sem, msg_send, msg_recv, taps_send, taps_recv, tail_send, hist_send, hist_recv,
    edge_send, edge_recv, p_send, p_recv, f_send, f_recv, out_send, out_recv,
):
    section = lax.axis_index("section")
    me = lax.axis_index("ctx")
    rows_of = n_ctx // 2
    z, x = me // 2, me % 2
    partner = me + 1 - 2 * x
    after = lax.rem(section + 1, n_section)
    before = lax.rem(section + n_section - 1, n_section)
    block, channels = q_ref.shape
    width = channels // n_ctx
    half = channels // 2

    sub = p_out.shape[2]
    parts = width // sub

    loads = [
        pltpu.make_async_copy(src, dst, load_sem.at[i])
        for i, (src, dst) in enumerate(
            (
                (short_hbm, short_ref), (prior_hbm, prior_ref), (gain_hbm, gain_ref),
                (tail_hbm, tail_ref), (k_hbm, k_ref), (v_hbm, v_ref), (q_hbm, q_ref),
                (taps_hbm.at[0], taps_all.at[z]), (fwd_hbm, fwd_f32), (inv_hbm, inv_f32),
            )
        )
    ]
    for load in loads:
        load.start()

    barrier = pltpu.get_barrier_semaphore()
    for step in range(1, n_ctx):
        pl.semaphore_signal(
            barrier, inc=1, device_id={"ctx": lax.rem(me + step, n_ctx)}, device_id_type=MESH
        )
    for other in (after, before):
        pl.semaphore_signal(barrier, inc=1, device_id={"section": other}, device_id_type=MESH)

    for load in loads[:4]:
        load.wait()
    pieces = [short_ref[0, m].astype(F32) for m in range(3)]
    pieces += [prior_ref[0, m].astype(F32) for m in range(3)]
    pieces.append(gain_ref[...].astype(F32))
    own_msg[...] = jnp.concatenate(pieces, axis=0).astype(BF16)
    msgs[me] = own_msg[...]
    tail = jnp.concatenate(
        [jnp.zeros((1, width), F32), tail_ref[0].astype(F32)], axis=0
    ).astype(BF16)
    for part in range(parts):
        own_tail[part] = tail[:, part * sub : (part + 1) * sub]

    @pl.when(z == 0)
    def _():
        for part in range(parts):
            hist[part] = own_tail[part]

    for load in loads[4:7]:
        load.wait()
    last = [ref[block - 16:, :].astype(F32)[14:] for ref in (q_ref, k_ref, v_ref)]
    edge_out[...] = jnp.concatenate(
        [piece[:, :half] for piece in last]
        + [piece[:, half:] for piece in last]
        + [jnp.zeros((4, half), F32)],
        axis=0,
    ).astype(BF16)

    pl.semaphore_wait(barrier, n_ctx + 1)

    def remote(src, dst, send, recv, **where):
        return pltpu.make_async_remote_copy(
            src_ref=src, dst_ref=dst, send_sem=send, recv_sem=recv,
            device_id=where, device_id_type=MESH,
        )

    chunks = rows_of * parts
    partner_step = lax.rem(partner - me + n_ctx, n_ctx)

    def edge_copy():
        return remote(edge_out, edge_in, edge_send, edge_recv, ctx=lax.rem(me + 1, n_ctx))

    def msg_copy(step, slot):
        return remote(
            own_msg, msgs.at[slot], msg_send.at[step], msg_recv.at[step],
            ctx=lax.rem(me + step, n_ctx),
        )

    def taps_copy(src, owner, up):
        return remote(
            src, taps_all.at[owner], taps_send.at[int(up), owner], taps_recv.at[owner],
            ctx=lax.rem(me + (2 if up else n_ctx - 2), n_ctx),
        )

    def tail_copy(part):
        slot = z * parts + part
        return remote(
            own_tail.at[part], hist.at[slot], tail_send.at[part], hist_recv.at[slot], ctx=x
        )

    def hist_copy(src, i):
        return remote(
            src.at[i], hist.at[i], hist_send.at[i], hist_recv.at[i],
            ctx=lax.rem(me + 2, n_ctx),
        )

    def p_copy(i):
        return remote(p_out.at[i], p_in.at[i], p_send.at[i], p_recv.at[i], ctx=partner)

    def f_copy(i):
        return remote(f_out.at[i], f_in.at[i], f_send.at[i], f_recv.at[i], ctx=partner)

    def columns(c):
        return pl.ds(pl.multiple_of(c * width, 128), width)

    def out_copy(t):
        at = pl.ds(pl.multiple_of(t * sub, 128), sub)
        return remote(
            mixed.at[:, at], out_ref.at[:, at], out_send.at[t], out_recv.at[t], section=after
        )

    def chunk(n, at=z):
        step = n // parts
        row = jnp.where(step < rows_of - at, at + step, rows_of - 1 - step)
        part = lax.rem(n, parts)
        return row * parts + part, row, part

    @pl.when(me < n_ctx - 1)
    def _():
        edge_copy().start()

    msg_copy(partner_step, me).start()
    for step in range(n_ctx - 1, 0, -1):

        @pl.when(step != partner_step)
        def _():
            msg_copy(step, me).start()

    @pl.when(z < rows_of - 1)
    def _():
        taps_copy(taps_hbm.at[0], z, True).start()

    @pl.when(z > 0)
    def _():
        taps_copy(taps_hbm.at[0], z, False).start()

    @pl.when(z > 0)
    def _():
        for part in range(parts):
            tail_copy(part).start()

    def wait_msg(c):
        @pl.when(c != me)
        def _():
            msg_copy(lax.rem(me - c + n_ctx, n_ctx), c).wait_recv()

    @pl.when(me > 0)
    def _():
        edge_copy().wait_recv()
        got = edge_in[...].astype(F32)
        edges[0:6, :half] = got[0:6]
        edges[0:6, half:] = got[6:12]

    def place_edge(c):
        @pl.when(me == 0)
        def _():
            edges[0:6, columns(c)] = msgs[c].astype(F32)[9:15]

    def feature(ref, at, m, weights):
        rows = ref[:, at].astype(F32)
        ends = edges[0:6, at]
        older, newer = ends[2 * m : 2 * m + 1], ends[2 * m + 1 : 2 * m + 2]
        place = lax.broadcasted_iota(jnp.int32, rows.shape, 0)
        one = jnp.where(place == 0, newer, pltpu.roll(rows, 1, 0))
        two = jnp.where(
            place == 0, older, jnp.where(place == 1, newer, pltpu.roll(rows, 2, 0))
        )
        taps = weights[3 * m : 3 * m + 3]
        return taps[0:1] * rows + taps[1:2] * one + taps[2:3] * two

    def lanes(c, part):
        for lane in range(0, sub, 128):
            inside = pl.ds(pl.multiple_of(part * sub + lane, 128), 128)
            at = pl.ds(pl.multiple_of(c * width + part * sub + lane, 128), 128)
            yield lane, at, msgs[c, :, inside].astype(F32)

    def product(c, part, dst, slot):
        for lane, at, weights in lanes(c, part):
            key = feature(k_ref, at, 1, weights)
            value = feature(v_ref, at, 2, weights)
            dst[slot, :, lane : lane + 128] = (key * value).astype(BF16)

    def partner_products(n, carry):
        slot, row, part = chunk(n)
        c = 2 * row + 1 - x

        @pl.when(part == 0)
        def _():
            wait_msg(c)
            place_edge(c)

        product(c, part, p_out, slot)
        p_copy(slot).start()
        return carry

    lax.fori_loop(0, chunks, partner_products, 0)

    def own_products(n, carry):
        slot, row, part = chunk(n, jnp.minimum(z + 1, rows_of - 1))
        c = 2 * row + x

        @pl.when(part == 0)
        def _():
            wait_msg(c)
            place_edge(c)

        product(c, part, p_own, slot)

        @pl.when((x == 1) & (z < rows_of - 1))
        def _():
            hist_copy(p_own, slot).start()

        return carry

    lax.fori_loop(0, chunks, own_products, 0)
    for load in loads[7:]:
        load.wait()
    fwd_ref[0], fwd_ref[1] = two_terms(fwd_f32[...])
    inv_ref[0], inv_ref[1] = two_terms(inv_f32[...])

    def finish(c, part, filtered):
        for lane, at, weights in lanes(c, part):
            query = feature(q_ref, at, 0, weights)
            mixed[:, at] = (query * filtered[:, lane : lane + 128]).astype(BF16)
        out_copy(c * parts + part).start()

    def from_partner(n):
        slot, row, part = chunk(n)
        f_copy(slot).wait_recv()
        finish(2 * row + 1 - x, part, f_in[slot].astype(F32))

    def spectrum(window):
        return dot(fwd_ref[0], window) + dot(fwd_ref[1], window)

    def filtered_block(slot, before_ref, current_ref):
        window = jnp.concatenate([before_ref[slot], current_ref[slot]], axis=0)
        waves = spectrum(window)
        one, two = waves[:block], waves[block:]
        real, imag = responses[slot, :block], responses[slot, block:]
        result = jnp.concatenate([one * real - two * imag, one * imag + two * real], axis=0)
        high, low = two_terms(result)
        return dot(inv_ref[0], high) + (dot(inv_ref[1], high) + dot(inv_ref[0], low))

    def give_back(slot, before_ref):
        f_out[slot] = filtered_block(slot, before_ref, p_in).astype(BF16)
        f_copy(slot).start()

    def keep(n, before_ref):
        slot, row, part = chunk(n)
        finish(2 * row + x, part, filtered_block(slot, before_ref, p_own))

    def wait_hist(slot):
        @pl.when((z > 0) | (slot >= parts))
        def _():
            hist_copy(p_own, slot).wait_recv()

    def relay(step):
        below, above = z - step, z + step

        @pl.when(below >= 0)
        def _():
            taps_copy(taps_all.at[below], below, True).wait_recv()

            @pl.when(z < rows_of - 1)
            def _():
                taps_copy(taps_all.at[below], below, True).start()

        @pl.when(above < rows_of)
        def _():
            taps_copy(taps_all.at[above], above, False).wait_recv()

            @pl.when(z > 0)
            def _():
                taps_copy(taps_all.at[above], above, False).start()

    def respond(n):
        slot, row, part = chunk(n)
        at = pl.ds(pl.multiple_of(part * sub, 128), sub)
        taps = taps_all[row, at, :]
        over = (((1,), (1,)), ((), ()))
        response = lax.dot_general(
            fwd_ref[0, :, :block], taps, over, preferred_element_type=F32
        ) + lax.dot_general(fwd_ref[1, :, :block], taps, over, preferred_element_type=F32)
        gain = msgs[2 * row + x, :, at].astype(F32)[15:16]
        responses[slot, :block] = response[:block] + gain
        responses[slot, block:] = response[block:]

    def with_product(n, carry):
        slot, _, part = chunk(n)
        p_copy(slot).wait_recv()

        @pl.when((x == 0) & (z < rows_of - 1))
        def _():
            hist_copy(p_in, slot).start()

        @pl.when((n >= parts) & (part == 0))
        def _():
            relay(n // parts)

        respond(n)

        @pl.when(x == 0)
        def _():
            give_back(slot, p_own)

        @pl.when(x == 1)
        def _():
            keep(n, p_in)

            @pl.when(n > 0)
            def _():
                with_history(n - 1)

        return carry

    def with_history(n):
        slot, _, _ = chunk(n)
        wait_hist(slot)
        give_back(slot, hist)

    def own_rows(n, carry):
        slot, _, _ = chunk(n)

        wait_hist(slot)
        keep(n, hist)
        return carry

    def with_partner(n, carry):
        from_partner(n)
        return carry

    lax.fori_loop(0, chunks, with_product, 0)

    @pl.when(x == 1)
    def _():
        with_history(chunks - 1)

    @pl.when(x == 0)
    def _():
        lax.fori_loop(0, chunks, own_rows, 0)

    lax.fori_loop(0, chunks, with_partner, 0)

    @pl.when(me < n_ctx - 1)
    def _():
        edge_copy().wait_send()

    for step in range(1, n_ctx):
        msg_copy(step, me).wait_send()

    def drain_taps(owner, carry):
        @pl.when((owner <= z) & (z < rows_of - 1))
        def _():
            taps_copy(taps_all.at[owner], owner, True).wait_send()

        @pl.when((owner >= z) & (z > 0))
        def _():
            taps_copy(taps_all.at[owner], owner, False).wait_send()

        return carry

    lax.fori_loop(0, rows_of, drain_taps, 0)

    @pl.when(z > 0)
    def _():
        for part in range(parts):
            tail_copy(part).wait_send()

    def drain(i, carry):
        p_copy(i).wait_send()
        f_copy(i).wait_send()

        @pl.when(z < rows_of - 1)
        def _():
            hist_copy(p_own, i).wait_send()

        return carry

    lax.fori_loop(0, chunks, drain, 0)

    def drain_out(t, carry):
        out_copy(t).wait()
        return carry

    lax.fori_loop(0, 2 * chunks, drain_out, 0)


def body(n_section, n_ctx, query, key, value, short_taps, long_taps, skip_gain, prior_qkv, prior_product):
    block, channels = query.shape
    width = channels // n_ctx
    rows_of = n_ctx // 2
    forward, inverse = transforms(block)
    hbm = pl.BlockSpec(memory_space=pltpu.HBM)
    sub = min(width, CHUNK)
    chunks = rows_of * width // sub
    slots = (chunks, block, sub)
    sems = pltpu.SemaphoreType.DMA
    return pl.pallas_call(
        functools.partial(kernel, n_section, n_ctx),
        out_shape=jax.ShapeDtypeStruct(query.shape, BF16),
        in_specs=[hbm] * 10,
        out_specs=pl.BlockSpec(memory_space=pl.ANY),
        scratch_shapes=[
            pltpu.VMEM((block, channels), BF16),
            pltpu.VMEM((block, channels), BF16),
            pltpu.VMEM((block, channels), BF16),
            pltpu.VMEM(short_taps.shape, BF16),
            pltpu.VMEM(skip_gain.shape, BF16),
            pltpu.VMEM(prior_qkv.shape, BF16),
            pltpu.VMEM(prior_product.shape, BF16),
            pltpu.VMEM(forward.shape, F32),
            pltpu.VMEM(inverse.shape, F32),
            pltpu.VMEM((2,) + forward.shape, BF16),
            pltpu.VMEM((2,) + inverse.shape, BF16),
            pltpu.VMEM((16, width), BF16),
            pltpu.VMEM((n_ctx, 16, width), BF16),
            pltpu.VMEM((rows_of, width, block), BF16),
            pltpu.VMEM((width // sub, block, sub), BF16),
            pltpu.VMEM((16, channels // 2), BF16),
            pltpu.VMEM((16, channels // 2), BF16),
            pltpu.VMEM((8, channels), F32),
            pltpu.VMEM(slots, BF16),
            pltpu.VMEM(slots, BF16),
            pltpu.VMEM(slots, BF16),
            pltpu.VMEM(slots, BF16),
            pltpu.VMEM((chunks, 2 * block, sub), F32),
            pltpu.VMEM(slots, BF16),
            pltpu.VMEM(slots, BF16),
            pltpu.VMEM((block, channels), BF16),
            sems((10,)),
            sems((n_ctx,)),
            sems((n_ctx,)),
            sems((2, rows_of)),
            sems((rows_of,)),
            sems((width // sub,)),
            sems((chunks,)),
            sems((chunks,)),
            sems,
            sems,
            sems((chunks,)),
            sems((chunks,)),
            sems((chunks,)),
            sems((chunks,)),
            sems((2 * chunks,)),
            sems((2 * chunks,)),
        ],
        compiler_params=pltpu.CompilerParams(
            collective_id=0, has_side_effects=True, vmem_limit_bytes=VMEM_BYTES
        ),
        cost_estimate=pl.CostEstimate(
            flops=2 * 2 * 256 * 256 * 4096, bytes_accessed=6 * 2**20, transcendentals=0
        ),
        name="paired_filter",
    )(
        query, key, value, short_taps, long_taps, skip_gain, prior_qkv, prior_product,
        jnp.asarray(forward), jnp.asarray(inverse),
    )


def solution(mesh):
    in_specs = (
        P(("section", "ctx"), None),
        P(("section", "ctx"), None),
        P(("section", "ctx"), None),
        P("section", None, None, "ctx"),
        P("section", "ctx", None),
        P("section", "ctx"),
        P("section", None, None, "ctx"),
        P("section", None, "ctx"),
    )
    out_specs = P(("section", "ctx"), None)
    run = functools.partial(body, mesh.shape["section"], mesh.shape["ctx"])
    return jax.shard_map(run, mesh=mesh, in_specs=in_specs, out_specs=out_specs, check_vma=False)
```

```python
import functools

import jax
import jax.numpy as jnp
import numpy as np
from jax import lax
from jax.experimental import pallas as pl
from jax.experimental.pallas import tpu as pltpu
from jax.sharding import PartitionSpec as P

MESH = pl.DeviceIdType.MESH
F32 = jnp.float32
BF16 = jnp.bfloat16
CHUNK = 512
VMEM_BYTES = 62 * 1024 * 1024


def transforms(block):
    size = 2 * block
    freq = (2 * np.arange(block)[:, None] + 1).astype(np.int64)
    turn = np.pi * ((freq * np.arange(size)[None, :]) % (2 * size)) / size
    forward = np.concatenate([np.cos(turn), -np.sin(turn)], axis=0)
    inverse = (forward * (2.0 / size)).T[block:]

    return forward.astype(np.float32), inverse.astype(np.float32)


def two_terms(matrix):
    high = matrix.astype(BF16)
    return high, (matrix - high.astype(F32)).astype(BF16)


def dot(a, b):
    return jnp.dot(a, b, preferred_element_type=F32)


def kernel(
    n_section, n_ctx,
    q_hbm, k_hbm, v_hbm, short_hbm, taps_hbm, gain_hbm, prior_hbm, tail_hbm, fwd_hbm, inv_hbm,
    out_ref,
    q_ref, k_ref, v_ref, short_ref, gain_ref, prior_ref, tail_ref, fwd_f32, inv_f32, fwd_ref, resp_ref, inv_ref, own_msg, msgs, taps_all, own_tail, edge_out, edge_in, edges,
    p_out, p_own, p_in, hist, responses, f_out, f_in, mixed,
    load_sem, msg_send, msg_recv, taps_send, taps_recv, tail_send, hist_send, hist_recv,
    edge_send, edge_recv, p_send, p_recv, f_send, f_recv, out_send, out_recv,
):
    section = lax.axis_index("section")
    me = lax.axis_index("ctx")
    rows_of = n_ctx // 2
    z, x = me // 2, me % 2
    partner = me + 1 - 2 * x
    after = lax.rem(section + 1, n_section)
    before = lax.rem(section + n_section - 1, n_section)
    block, channels = q_ref.shape
    width = channels // n_ctx
    half = channels // 2

    sub = p_out.shape[2]
    parts = width // sub

    loads = [
        pltpu.make_async_copy(src, dst, load_sem.at[i])
        for i, (src, dst) in enumerate(
            (
                (short_hbm, short_ref), (prior_hbm, prior_ref), (gain_hbm, gain_ref),
                (tail_hbm, tail_ref), (k_hbm, k_ref), (v_hbm, v_ref), (q_hbm, q_ref),
                (taps_hbm.at[0], taps_all.at[z]), (fwd_hbm, fwd_f32), (inv_hbm, inv_f32),
            )
        )
    ]
    for load in loads:
        load.start()

    barrier = pltpu.get_barrier_semaphore()
    for step in range(1, n_ctx):
        pl.semaphore_signal(
            barrier, inc=1, device_id={"ctx": lax.rem(me + step, n_ctx)}, device_id_type=MESH
        )
    for other in (after, before):
        pl.semaphore_signal(barrier, inc=1, device_id={"section": other}, device_id_type=MESH)

    for load in loads[:4]:
        load.wait()
    pieces = [short_ref[0, m].astype(F32) for m in range(3)]
    pieces += [prior_ref[0, m].astype(F32) for m in range(3)]
    pieces.append(gain_ref[...].astype(F32))
    own_msg[...] = jnp.concatenate(pieces, axis=0).astype(BF16)
    msgs[me] = own_msg[...]
    tail = jnp.concatenate(
        [jnp.zeros((1, width), F32), tail_ref[0].astype(F32)], axis=0
    ).astype(BF16)
    for part in range(parts):
        own_tail[part] = tail[:, part * sub : (part + 1) * sub]

    @pl.when(z == 0)
    def _():
        for part in range(parts):
            hist[part] = own_tail[part]

    for load in loads[4:7]:
        load.wait()
    last = [ref[block - 16:, :].astype(F32)[14:] for ref in (q_ref, k_ref, v_ref)]
    edge_out[...] = jnp.concatenate(
        [piece[:, :half] for piece in last]
        + [piece[:, half:] for piece in last]
        + [jnp.zeros((4, half), F32)],
        axis=0,
    ).astype(BF16)

    pl.semaphore_wait(barrier, n_ctx + 1)

    def remote(src, dst, send, recv, **where):
        return pltpu.make_async_remote_copy(
            src_ref=src, dst_ref=dst, send_sem=send, recv_sem=recv,
            device_id=where, device_id_type=MESH,
        )

    chunks = rows_of * parts
    partner_step = lax.rem(partner - me + n_ctx, n_ctx)

    def edge_copy():
        return remote(edge_out, edge_in, edge_send, edge_recv, ctx=lax.rem(me + 1, n_ctx))

    def msg_copy(step, slot):
        return remote(
            own_msg, msgs.at[slot], msg_send.at[step], msg_recv.at[step],
            ctx=lax.rem(me + step, n_ctx),
        )

    def taps_copy(src, owner, up):
        return remote(
            src, taps_all.at[owner], taps_send.at[int(up), owner], taps_recv.at[owner],
            ctx=lax.rem(me + (2 if up else n_ctx - 2), n_ctx),
        )

    def tail_copy(part):
        slot = z * parts + part
        return remote(
            own_tail.at[part], hist.at[slot], tail_send.at[part], hist_recv.at[slot], ctx=x
        )

    def hist_copy(src, i):
        return remote(
            src.at[i], hist.at[i], hist_send.at[i], hist_recv.at[i],
            ctx=lax.rem(me + 2, n_ctx),
        )

    def p_copy(i):
        return remote(p_out.at[i], p_in.at[i], p_send.at[i], p_recv.at[i], ctx=partner)

    def f_copy(i):
        return remote(f_out.at[i], f_in.at[i], f_send.at[i], f_recv.at[i], ctx=partner)

    def columns(c):
        return pl.ds(pl.multiple_of(c * width, 128), width)

    def out_copy(t):
        at = pl.ds(pl.multiple_of(t * sub, 128), sub)
        return remote(
            mixed.at[:, at], out_ref.at[:, at], out_send.at[t], out_recv.at[t], section=after
        )

    def chunk(n, at=z):
        step = n // parts
        row = jnp.where(step < rows_of - at, at + step, rows_of - 1 - step)
        part = lax.rem(n, parts)
        return row * parts + part, row, part

    @pl.when(me < n_ctx - 1)
    def _():
        edge_copy().start()

    msg_copy(partner_step, me).start()
    for step in range(n_ctx - 1, 0, -1):

        @pl.when(step != partner_step)
        def _():
            msg_copy(step, me).start()

    @pl.when(z < rows_of - 1)
    def _():
        taps_copy(taps_hbm.at[0], z, True).start()

    @pl.when(z > 0)
    def _():
        taps_copy(taps_hbm.at[0], z, False).start()

    @pl.when(z > 0)
    def _():
        for part in range(parts):
            tail_copy(part).start()

    def respond(n):
        slot, row, part = chunk(n)
        at = pl.ds(pl.multiple_of(part * sub, 128), sub)
        taps = taps_all[row, at, :]
        response = lax.dot_general(
            resp_ref[...],
            jnp.concatenate([taps, taps], axis=1),
            (((1,), (1,)), ((), ())),
            preferred_element_type=F32,
        )
        gain = msgs[2 * row + x, :, at].astype(F32)[15:16]
        responses[slot, :block] = response[:block] + gain
        responses[slot, block:] = response[block:]

    for load in loads[7:]:
        load.wait()
    high, low = two_terms(fwd_f32[...])
    fwd_ref[...] = jnp.concatenate([high, low], axis=1)
    resp_ref[...] = jnp.concatenate([high[:, :block], low[:, :block]], axis=1)
    high, low = two_terms(inv_f32[...])
    inv_ref[...] = jnp.concatenate([high, low, high], axis=1)
    for part in range(parts):
        respond(part)

    def wait_msg(c):
        @pl.when(c != me)
        def _():
            msg_copy(lax.rem(me - c + n_ctx, n_ctx), c).wait_recv()

    @pl.when(me > 0)
    def _():
        edge_copy().wait_recv()
        got = edge_in[...].astype(F32)
        edges[0:6, :half] = got[0:6]
        edges[0:6, half:] = got[6:12]

    def place_edge(c):
        @pl.when(me == 0)
        def _():
            edges[0:6, columns(c)] = msgs[c].astype(F32)[9:15]

    def feature(ref, at, m, weights):
        rows = ref[:, at].astype(F32)
        ends = edges[0:6, at]
        older, newer = ends[2 * m : 2 * m + 1], ends[2 * m + 1 : 2 * m + 2]
        one, two = pltpu.roll(rows, 1, 0), pltpu.roll(rows, 2, 0)
        place = lax.broadcasted_iota(jnp.int32, (8, 128), 0)
        first = jnp.where(place == 0, newer, one[:8])
        second = jnp.where(place == 0, older, jnp.where(place == 1, newer, two[:8]))
        one = jnp.concatenate([first, one[8:]], axis=0)
        two = jnp.concatenate([second, two[8:]], axis=0)
        taps = weights[3 * m : 3 * m + 3]
        return taps[0:1] * rows + taps[1:2] * one + taps[2:3] * two

    def lanes(c, part):
        for lane in range(0, sub, 128):
            inside = pl.ds(pl.multiple_of(part * sub + lane, 128), 128)
            at = pl.ds(pl.multiple_of(c * width + part * sub + lane, 128), 128)
            yield lane, at, msgs[c, :, inside].astype(F32)

    def product(c, part, dst, slot):
        for lane, at, weights in lanes(c, part):
            key = feature(k_ref, at, 1, weights)
            value = feature(v_ref, at, 2, weights)
            dst[slot, :, lane : lane + 128] = (key * value).astype(BF16)

    def partner_products(n, carry):
        slot, row, part = chunk(n)
        c = 2 * row + 1 - x

        @pl.when(part == 0)
        def _():
            wait_msg(c)
            place_edge(c)

        product(c, part, p_out, slot)
        p_copy(slot).start()
        return carry

    lax.fori_loop(0, chunks, partner_products, 0)

    def own_products(n, carry):
        slot, row, part = chunk(n, jnp.minimum(z + 1, rows_of - 1))
        c = 2 * row + x

        @pl.when(part == 0)
        def _():
            wait_msg(c)
            place_edge(c)

        product(c, part, p_own, slot)

        @pl.when((x == 1) & (z < rows_of - 1))
        def _():
            hist_copy(p_own, slot).start()

        return carry

    lax.fori_loop(0, chunks, own_products, 0)

    def finish(c, part, filtered):
        for lane, at, weights in lanes(c, part):
            query = feature(q_ref, at, 0, weights)
            mixed[:, at] = (query * filtered[:, lane : lane + 128]).astype(BF16)
        out_copy(c * parts + part).start()

    def from_partner(n):
        slot, row, part = chunk(n)
        f_copy(slot).wait_recv()
        finish(2 * row + 1 - x, part, f_in[slot].astype(F32))

    def filtered_block(slot, before_ref, current_ref):
        window = [before_ref[slot], current_ref[slot]]
        waves = dot(fwd_ref[...], jnp.concatenate(window + window, axis=0))
        one, two = waves[:block], waves[block:]
        real, imag = responses[slot, :block], responses[slot, block:]
        result = jnp.concatenate([one * real - two * imag, one * imag + two * real], axis=0)
        high, low = two_terms(result)
        return dot(inv_ref[...], jnp.concatenate([high, high, low], axis=0))

    def give_back(slot, before_ref):
        f_out[slot] = filtered_block(slot, before_ref, p_in).astype(BF16)
        f_copy(slot).start()

    def keep(n, before_ref):
        slot, row, part = chunk(n)
        finish(2 * row + x, part, filtered_block(slot, before_ref, p_own))

    def wait_hist(slot):
        @pl.when((z > 0) | (slot >= parts))
        def _():
            hist_copy(p_own, slot).wait_recv()

    def relay(step):
        below, above = z - step, z + step

        @pl.when(below >= 0)
        def _():
            taps_copy(taps_all.at[below], below, True).wait_recv()

            @pl.when(z < rows_of - 1)
            def _():
                taps_copy(taps_all.at[below], below, True).start()

        @pl.when(above < rows_of)
        def _():
            taps_copy(taps_all.at[above], above, False).wait_recv()

            @pl.when(z > 0)
            def _():
                taps_copy(taps_all.at[above], above, False).start()

    def with_product(n, carry):
        slot, _, part = chunk(n)
        p_copy(slot).wait_recv()

        @pl.when((x == 0) & (z < rows_of - 1))
        def _():
            hist_copy(p_in, slot).start()

        @pl.when((n >= parts) & (part == 0))
        def _():
            relay(n // parts)

        @pl.when(n >= parts)
        def _():
            respond(n)

        @pl.when(x == 0)
        def _():
            give_back(slot, p_own)

        @pl.when(x == 1)
        def _():
            keep(n, p_in)

            @pl.when(n > 0)
            def _():
                with_history(n - 1)

        return carry

    def with_history(n):
        slot, _, _ = chunk(n)
        wait_hist(slot)
        give_back(slot, hist)

    def own_rows(n, carry):
        slot, _, _ = chunk(n)

        wait_hist(slot)
        keep(n, hist)
        return carry

    def with_partner(n, carry):
        from_partner(n)
        return carry

    lax.fori_loop(0, chunks, with_product, 0)

    @pl.when(x == 1)
    def _():
        with_history(chunks - 1)

    @pl.when(x == 0)
    def _():
        lax.fori_loop(0, chunks, own_rows, 0)

    lax.fori_loop(0, chunks, with_partner, 0)

    @pl.when(me < n_ctx - 1)
    def _():
        edge_copy().wait_send()

    for step in range(1, n_ctx):
        msg_copy(step, me).wait_send()

    def drain_taps(owner, carry):
        @pl.when((owner <= z) & (z < rows_of - 1))
        def _():
            taps_copy(taps_all.at[owner], owner, True).wait_send()

        @pl.when((owner >= z) & (z > 0))
        def _():
            taps_copy(taps_all.at[owner], owner, False).wait_send()

        return carry

    lax.fori_loop(0, rows_of, drain_taps, 0)

    @pl.when(z > 0)
    def _():
        for part in range(parts):
            tail_copy(part).wait_send()

    def drain(i, carry):
        p_copy(i).wait_send()
        f_copy(i).wait_send()

        @pl.when(z < rows_of - 1)
        def _():
            hist_copy(p_own, i).wait_send()

        return carry

    lax.fori_loop(0, chunks, drain, 0)

    def drain_out(t, carry):
        out_copy(t).wait()
        return carry

    lax.fori_loop(0, 2 * chunks, drain_out, 0)


def body(n_section, n_ctx, query, key, value, short_taps, long_taps, skip_gain, prior_qkv, prior_product):
    block, channels = query.shape
    width = channels // n_ctx
    rows_of = n_ctx // 2
    forward, inverse = transforms(block)
    hbm = pl.BlockSpec(memory_space=pltpu.HBM)
    sub = min(width, CHUNK)
    chunks = rows_of * width // sub
    slots = (chunks, block, sub)
    sems = pltpu.SemaphoreType.DMA
    return pl.pallas_call(
        functools.partial(kernel, n_section, n_ctx),
        out_shape=pltpu.VMEM(query.shape, BF16),
        in_specs=[hbm] * 10,
        out_specs=pl.BlockSpec(memory_space=pl.ANY),
        scratch_shapes=[
            pltpu.VMEM((block, channels), BF16),
            pltpu.VMEM((block, channels), BF16),
            pltpu.VMEM((block, channels), BF16),
            pltpu.VMEM(short_taps.shape, BF16),
            pltpu.VMEM(skip_gain.shape, BF16),
            pltpu.VMEM(prior_qkv.shape, BF16),
            pltpu.VMEM(prior_product.shape, BF16),
            pltpu.VMEM(forward.shape, F32),
            pltpu.VMEM(inverse.shape, F32),
            pltpu.VMEM((2 * block, 4 * block), BF16),
            pltpu.VMEM((2 * block, 2 * block), BF16),
            pltpu.VMEM((block, 6 * block), BF16),
            pltpu.VMEM((16, width), BF16),
            pltpu.VMEM((n_ctx, 16, width), BF16),
            pltpu.VMEM((rows_of, width, block), BF16),
            pltpu.VMEM((width // sub, block, sub), BF16),
            pltpu.VMEM((16, channels // 2), BF16),
            pltpu.VMEM((16, channels // 2), BF16),
            pltpu.VMEM((8, channels), F32),
            pltpu.VMEM(slots, BF16),
            pltpu.VMEM(slots, BF16),
            pltpu.VMEM(slots, BF16),
            pltpu.VMEM(slots, BF16),
            pltpu.VMEM((chunks, 2 * block, sub), F32),
            pltpu.VMEM(slots, BF16),
            pltpu.VMEM(slots, BF16),
            pltpu.VMEM((block, channels), BF16),
            sems((10,)),
            sems((n_ctx,)),
            sems((n_ctx,)),
            sems((2, rows_of)),
            sems((rows_of,)),
            sems((width // sub,)),
            sems((chunks,)),
            sems((chunks,)),
            sems,
            sems,
            sems((chunks,)),
            sems((chunks,)),
            sems((chunks,)),
            sems((chunks,)),
            sems((2 * chunks,)),
            sems((2 * chunks,)),
        ],
        compiler_params=pltpu.CompilerParams(
            collective_id=0, has_side_effects=True, vmem_limit_bytes=VMEM_BYTES
        ),
        cost_estimate=pl.CostEstimate(
            flops=2 * 2 * 256 * 256 * 4096, bytes_accessed=6 * 2**20, transcendentals=0
        ),
        name="paired_filter",
    )(
        query, key, value, short_taps, long_taps, skip_gain, prior_qkv, prior_product,
        jnp.asarray(forward), jnp.asarray(inverse),
    )


def solution(mesh):
    in_specs = (
        P(("section", "ctx"), None),
        P(("section", "ctx"), None),
        P(("section", "ctx"), None),
        P("section", None, None, "ctx"),
        P("section", "ctx", None),
        P("section", "ctx"),
        P("section", None, None, "ctx"),
        P("section", None, "ctx"),
    )
    out_specs = P(("section", "ctx"), None)
    run = functools.partial(body, mesh.shape["section"], mesh.shape["ctx"])
    return jax.shard_map(run, mesh=mesh, in_specs=in_specs, out_specs=out_specs, check_vma=False)
```

```python
import functools

import jax
import jax.numpy as jnp
import numpy as np
from jax import lax
from jax.experimental import pallas as pl
from jax.experimental.pallas import tpu as pltpu
from jax.sharding import PartitionSpec as P

MESH = pl.DeviceIdType.MESH
F32 = jnp.float32
BF16 = jnp.bfloat16
CHUNK = 512
VMEM_BYTES = 62 * 1024 * 1024


def transforms(block):
    size = 2 * block
    freq = (2 * np.arange(block)[:, None] + 1).astype(np.int64)
    turn = np.pi * ((freq * np.arange(size)[None, :]) % (2 * size)) / size
    forward = np.concatenate([np.cos(turn), -np.sin(turn)], axis=0)
    inverse = (forward * (2.0 / size)).T[block:]

    return forward.astype(np.float32), inverse.astype(np.float32)


def two_terms(matrix):
    high = matrix.astype(BF16)
    return high, (matrix - high.astype(F32)).astype(BF16)


def dot(a, b):
    return jnp.dot(a, b, preferred_element_type=F32)


def kernel(
    n_section, n_ctx,
    q_hbm, k_hbm, v_hbm, short_hbm, taps_hbm, gain_hbm, prior_hbm, tail_hbm, fwd_hbm, inv_hbm,
    out_ref,
    q_ref, k_ref, v_ref, short_ref, gain_ref, prior_ref, tail_ref, fwd_f32, inv_f32, fwd_ref, resp_ref, inv_ref, own_msg, msgs, taps_all, own_tail, edge_out, edge_in, edges,
    p_out, p_own, p_in, hist, responses, f_out, f_in, mixed,
    load_sem, msg_send, msg_recv, taps_send, taps_recv, tail_send, hist_send, hist_recv,
    edge_send, edge_recv, p_send, p_recv, f_send, f_recv, out_send, out_recv,
):
    section = lax.axis_index("section")
    me = lax.axis_index("ctx")
    rows_of = n_ctx // 2
    z, x = me // 2, me % 2
    partner = me + 1 - 2 * x
    after = lax.rem(section + 1, n_section)
    before = lax.rem(section + n_section - 1, n_section)
    block, channels = q_ref.shape
    width = channels // n_ctx
    half = channels // 2

    sub = p_out.shape[2]
    parts = width // sub

    loads = [
        pltpu.make_async_copy(src, dst, load_sem.at[i])
        for i, (src, dst) in enumerate(
            (
                (short_hbm, short_ref), (prior_hbm, prior_ref), (gain_hbm, gain_ref),
                (tail_hbm, tail_ref), (k_hbm, k_ref), (v_hbm, v_ref), (q_hbm, q_ref),
                (taps_hbm.at[0], taps_all.at[z]), (fwd_hbm, fwd_f32), (inv_hbm, inv_f32),
            )
        )
    ]
    for load in loads:
        load.start()

    barrier = pltpu.get_barrier_semaphore()
    for step in range(1, n_ctx):
        pl.semaphore_signal(
            barrier, inc=1, device_id={"ctx": lax.rem(me + step, n_ctx)}, device_id_type=MESH
        )
    for other in (after, before):
        pl.semaphore_signal(barrier, inc=1, device_id={"section": other}, device_id_type=MESH)

    for load in loads[:4]:
        load.wait()
    pieces = [short_ref[0, m].astype(F32) for m in range(3)]
    pieces += [prior_ref[0, m].astype(F32) for m in range(3)]
    pieces.append(gain_ref[...].astype(F32))
    own_msg[...] = jnp.concatenate(pieces, axis=0).astype(BF16)
    msgs[me] = own_msg[...]
    tail = jnp.concatenate(
        [jnp.zeros((1, width), F32), tail_ref[0].astype(F32)], axis=0
    ).astype(BF16)
    for part in range(parts):
        own_tail[part] = tail[:, part * sub : (part + 1) * sub]

    @pl.when(z == 0)
    def _():
        for part in range(parts):
            hist[part] = own_tail[part]

    for load in loads[4:7]:
        load.wait()
    last = [ref[block - 16:, :].astype(F32)[14:] for ref in (q_ref, k_ref, v_ref)]
    edge_out[...] = jnp.concatenate(
        [piece[:, :half] for piece in last]
        + [piece[:, half:] for piece in last]
        + [jnp.zeros((4, half), F32)],
        axis=0,
    ).astype(BF16)

    pl.semaphore_wait(barrier, n_ctx + 1)

    def remote(src, dst, send, recv, **where):
        return pltpu.make_async_remote_copy(
            src_ref=src, dst_ref=dst, send_sem=send, recv_sem=recv,
            device_id=where, device_id_type=MESH,
        )

    chunks = rows_of * parts

    def edge_copy():
        return remote(edge_out, edge_in, edge_send, edge_recv, ctx=lax.rem(me + 1, n_ctx))

    def msg_copy(src, owner, sem, target):
        return remote(src, msgs.at[owner], msg_send.at[sem], msg_recv.at[owner], ctx=target)

    def msg_copies(step):
        target = lax.rem(me + 2 * step, n_ctx)
        return (
            msg_copy(own_msg, me, step, target),
            msg_copy(msgs.at[partner], partner, rows_of - 1 + step, target),
        )

    def taps_copy(src, owner, up):
        return remote(
            src, taps_all.at[owner], taps_send.at[int(up), owner], taps_recv.at[owner],
            ctx=lax.rem(me + (2 if up else n_ctx - 2), n_ctx),
        )

    def tail_copy(part):
        slot = z * parts + part
        return remote(
            own_tail.at[part], hist.at[slot], tail_send.at[part], hist_recv.at[slot], ctx=x
        )

    def hist_copy(src, i):
        return remote(
            src.at[i], hist.at[i], hist_send.at[i], hist_recv.at[i],
            ctx=lax.rem(me + 2, n_ctx),
        )

    def p_copy(i):
        return remote(p_out.at[i], p_in.at[i], p_send.at[i], p_recv.at[i], ctx=partner)

    def f_copy(i):
        return remote(f_out.at[i], f_in.at[i], f_send.at[i], f_recv.at[i], ctx=partner)

    def columns(c):
        return pl.ds(pl.multiple_of(c * width, 128), width)

    def out_copy(t):
        at = pl.ds(pl.multiple_of(t * sub, 128), sub)
        return remote(
            mixed.at[:, at], out_ref.at[:, at], out_send.at[t], out_recv.at[t], section=after
        )

    def chunk(n, at=z):
        step = n // parts
        row = jnp.where(step < rows_of - at, at + step, rows_of - 1 - step)
        part = lax.rem(n, parts)
        return row * parts + part, row, part

    @pl.when(me < n_ctx - 1)
    def _():
        edge_copy().start()

    msg_copy(own_msg, me, 0, partner).start()
    for step in range(1, rows_of):
        msg_copies(step)[0].start()

    @pl.when(z < rows_of - 1)
    def _():
        taps_copy(taps_hbm.at[0], z, True).start()

    @pl.when(z > 0)
    def _():
        taps_copy(taps_hbm.at[0], z, False).start()

    @pl.when(z > 0)
    def _():
        for part in range(parts):
            tail_copy(part).start()

    def respond(n):
        slot, row, part = chunk(n)
        at = pl.ds(pl.multiple_of(part * sub, 128), sub)
        taps = taps_all[row, at, :]
        response = lax.dot_general(
            resp_ref[...],
            jnp.concatenate([taps, taps], axis=1),
            (((1,), (1,)), ((), ())),
            preferred_element_type=F32,
        )
        gain = msgs[2 * row + x, :, at].astype(F32)[15:16]
        responses[slot, :block] = response[:block] + gain
        responses[slot, block:] = response[block:]

    for load in loads[7:]:
        load.wait()
    high, low = two_terms(fwd_f32[...])
    fwd_ref[...] = jnp.concatenate([high, low], axis=1)
    resp_ref[...] = jnp.concatenate([high[:, :block], low[:, :block]], axis=1)
    high, low = two_terms(inv_f32[...])
    inv_ref[...] = jnp.concatenate([high, low, high], axis=1)
    for part in range(parts):
        respond(part)

    def wait_msg(c):
        @pl.when((c != me) & (c != partner))
        def _():
            msg_copy(own_msg, c, 0, partner).wait_recv()

    msg_copy(own_msg, partner, 0, partner).wait_recv()
    for step in range(1, rows_of):
        msg_copies(step)[1].start()

    @pl.when(me > 0)
    def _():
        edge_copy().wait_recv()
        got = edge_in[...].astype(F32)
        edges[0:6, :half] = got[0:6]
        edges[0:6, half:] = got[6:12]

    def place_edge(c):
        @pl.when(me == 0)
        def _():
            edges[0:6, columns(c)] = msgs[c].astype(F32)[9:15]

    def feature(ref, at, m, weights):
        rows = ref[:, at].astype(F32)
        ends = edges[0:6, at]
        older, newer = ends[2 * m : 2 * m + 1], ends[2 * m + 1 : 2 * m + 2]
        one, two = pltpu.roll(rows, 1, 0), pltpu.roll(rows, 2, 0)
        place = lax.broadcasted_iota(jnp.int32, (8, 128), 0)
        first = jnp.where(place == 0, newer, one[:8])
        second = jnp.where(place == 0, older, jnp.where(place == 1, newer, two[:8]))
        one = jnp.concatenate([first, one[8:]], axis=0)
        two = jnp.concatenate([second, two[8:]], axis=0)
        taps = weights[3 * m : 3 * m + 3]
        return taps[0:1] * rows + taps[1:2] * one + taps[2:3] * two

    def lanes(c, part):
        for lane in range(0, sub, 128):
            inside = pl.ds(pl.multiple_of(part * sub + lane, 128), 128)
            at = pl.ds(pl.multiple_of(c * width + part * sub + lane, 128), 128)
            yield lane, at, msgs[c, :, inside].astype(F32)

    def product(c, part, dst, slot):
        for lane, at, weights in lanes(c, part):
            key = feature(k_ref, at, 1, weights)
            value = feature(v_ref, at, 2, weights)
            dst[slot, :, lane : lane + 128] = (key * value).astype(BF16)

    def ready(c, part):
        @pl.when(part == 0)
        def _():
            wait_msg(c)
            place_edge(c)

    def products(n, carry):
        slot, row, part = chunk(n)
        c = 2 * row + 1 - x
        ready(c, part)
        product(c, part, p_out, slot)
        p_copy(slot).start()

        slot, row, part = chunk(n, jnp.minimum(z + 1, rows_of - 1))
        c = 2 * row + x
        ready(c, part)
        product(c, part, p_own, slot)

        @pl.when((x == 1) & (z < rows_of - 1))
        def _():
            hist_copy(p_own, slot).start()

        return carry

    lax.fori_loop(0, chunks, products, 0)

    def finish(c, part, filtered):
        for lane, at, weights in lanes(c, part):
            query = feature(q_ref, at, 0, weights)
            mixed[:, at] = (query * filtered[:, lane : lane + 128]).astype(BF16)
        out_copy(c * parts + part).start()

    def from_partner(n):
        slot, row, part = chunk(n)
        f_copy(slot).wait_recv()
        finish(2 * row + 1 - x, part, f_in[slot].astype(F32))

    def filtered_block(slot, before_ref, current_ref):
        window = [before_ref[slot], current_ref[slot]]
        waves = dot(fwd_ref[...], jnp.concatenate(window + window, axis=0))
        one, two = waves[:block], waves[block:]
        real, imag = responses[slot, :block], responses[slot, block:]
        result = jnp.concatenate([one * real - two * imag, one * imag + two * real], axis=0)
        high, low = two_terms(result)
        return dot(inv_ref[...], jnp.concatenate([high, high, low], axis=0))

    def give_back(slot, before_ref):
        f_out[slot] = filtered_block(slot, before_ref, p_in).astype(BF16)
        f_copy(slot).start()

    def keep(n, before_ref):
        slot, row, part = chunk(n)
        finish(2 * row + x, part, filtered_block(slot, before_ref, p_own))

    def wait_hist(slot):
        @pl.when((z > 0) | (slot >= parts))
        def _():
            hist_copy(p_own, slot).wait_recv()

    def relay(step):
        below, above = z - step, z + step

        @pl.when(below >= 0)
        def _():
            taps_copy(taps_all.at[below], below, True).wait_recv()

            @pl.when(z < rows_of - 1)
            def _():
                taps_copy(taps_all.at[below], below, True).start()

        @pl.when(above < rows_of)
        def _():
            taps_copy(taps_all.at[above], above, False).wait_recv()

            @pl.when(z > 0)
            def _():
                taps_copy(taps_all.at[above], above, False).start()

    def with_product(n, carry):
        slot, _, part = chunk(n)
        p_copy(slot).wait_recv()

        @pl.when((x == 0) & (z < rows_of - 1))
        def _():
            hist_copy(p_in, slot).start()

        @pl.when((n >= parts) & (part == 0))
        def _():
            relay(n // parts)

        @pl.when(n >= parts)
        def _():
            respond(n)

        @pl.when(x == 0)
        def _():
            give_back(slot, p_own)

        @pl.when(x == 1)
        def _():
            keep(n, p_in)

            @pl.when(n > 0)
            def _():
                with_history(n - 1)

        return carry

    def with_history(n):
        slot, _, _ = chunk(n)
        wait_hist(slot)
        give_back(slot, hist)

    def own_rows(n, carry):
        slot, _, _ = chunk(n)

        wait_hist(slot)
        keep(n, hist)
        return carry

    def with_partner(n, carry):
        from_partner(n)
        return carry

    lax.fori_loop(0, chunks, with_product, 0)

    @pl.when(x == 1)
    def _():
        with_history(chunks - 1)

    @pl.when(x == 0)
    def _():
        lax.fori_loop(0, chunks, own_rows, 0)

    lax.fori_loop(0, chunks, with_partner, 0)

    @pl.when(me < n_ctx - 1)
    def _():
        edge_copy().wait_send()

    msg_copy(own_msg, me, 0, partner).wait_send()
    for step in range(1, rows_of):
        for copy in msg_copies(step):
            copy.wait_send()

    def drain_taps(owner, carry):
        @pl.when((owner <= z) & (z < rows_of - 1))
        def _():
            taps_copy(taps_all.at[owner], owner, True).wait_send()

        @pl.when((owner >= z) & (z > 0))
        def _():
            taps_copy(taps_all.at[owner], owner, False).wait_send()

        return carry

    lax.fori_loop(0, rows_of, drain_taps, 0)

    @pl.when(z > 0)
    def _():
        for part in range(parts):
            tail_copy(part).wait_send()

    def drain(i, carry):
        p_copy(i).wait_send()
        f_copy(i).wait_send()

        @pl.when(z < rows_of - 1)
        def _():
            hist_copy(p_own, i).wait_send()

        return carry

    lax.fori_loop(0, chunks, drain, 0)

    def drain_out(t, carry):
        out_copy(t).wait()
        return carry

    lax.fori_loop(0, 2 * chunks, drain_out, 0)


def body(n_section, n_ctx, query, key, value, short_taps, long_taps, skip_gain, prior_qkv, prior_product):
    block, channels = query.shape
    width = channels // n_ctx
    rows_of = n_ctx // 2
    forward, inverse = transforms(block)
    hbm = pl.BlockSpec(memory_space=pltpu.HBM)
    sub = min(width, CHUNK)
    chunks = rows_of * width // sub
    slots = (chunks, block, sub)
    sems = pltpu.SemaphoreType.DMA
    return pl.pallas_call(
        functools.partial(kernel, n_section, n_ctx),
        out_shape=pltpu.VMEM(query.shape, BF16),
        in_specs=[hbm] * 10,
        out_specs=pl.BlockSpec(memory_space=pl.ANY),
        scratch_shapes=[
            pltpu.VMEM((block, channels), BF16),
            pltpu.VMEM((block, channels), BF16),
            pltpu.VMEM((block, channels), BF16),
            pltpu.VMEM(short_taps.shape, BF16),
            pltpu.VMEM(skip_gain.shape, BF16),
            pltpu.VMEM(prior_qkv.shape, BF16),
            pltpu.VMEM(prior_product.shape, BF16),
            pltpu.VMEM(forward.shape, F32),
            pltpu.VMEM(inverse.shape, F32),
            pltpu.VMEM((2 * block, 4 * block), BF16),
            pltpu.VMEM((2 * block, 2 * block), BF16),
            pltpu.VMEM((block, 6 * block), BF16),
            pltpu.VMEM((16, width), BF16),
            pltpu.VMEM((n_ctx, 16, width), BF16),
            pltpu.VMEM((rows_of, width, block), BF16),
            pltpu.VMEM((width // sub, block, sub), BF16),
            pltpu.VMEM((16, channels // 2), BF16),
            pltpu.VMEM((16, channels // 2), BF16),
            pltpu.VMEM((8, channels), F32),
            pltpu.VMEM(slots, BF16),
            pltpu.VMEM(slots, BF16),
            pltpu.VMEM(slots, BF16),
            pltpu.VMEM(slots, BF16),
            pltpu.VMEM((chunks, 2 * block, sub), F32),
            pltpu.VMEM(slots, BF16),
            pltpu.VMEM(slots, BF16),
            pltpu.VMEM((block, channels), BF16),
            sems((10,)),
            sems((n_ctx,)),
            sems((n_ctx,)),
            sems((2, rows_of)),
            sems((rows_of,)),
            sems((width // sub,)),
            sems((chunks,)),
            sems((chunks,)),
            sems,
            sems,
            sems((chunks,)),
            sems((chunks,)),
            sems((chunks,)),
            sems((chunks,)),
            sems((2 * chunks,)),
            sems((2 * chunks,)),
        ],
        compiler_params=pltpu.CompilerParams(
            collective_id=0, has_side_effects=True, vmem_limit_bytes=VMEM_BYTES
        ),
        cost_estimate=pl.CostEstimate(
            flops=2 * 2 * 256 * 256 * 4096, bytes_accessed=6 * 2**20, transcendentals=0
        ),
        name="paired_filter",
    )(
        query, key, value, short_taps, long_taps, skip_gain, prior_qkv, prior_product,
        jnp.asarray(forward), jnp.asarray(inverse),
    )


def solution(mesh):
    in_specs = (
        P(("section", "ctx"), None),
        P(("section", "ctx"), None),
        P(("section", "ctx"), None),
        P("section", None, None, "ctx"),
        P("section", "ctx", None),
        P("section", "ctx"),
        P("section", None, None, "ctx"),
        P("section", None, "ctx"),
    )
    out_specs = P(("section", "ctx"), None)
    run = functools.partial(body, mesh.shape["section"], mesh.shape["ctx"])
    return jax.shard_map(run, mesh=mesh, in_specs=in_specs, out_specs=out_specs, check_vma=False)
```
